32 devices in a mesh: prow: 4 (over z), pcol: 8 (over y, x, core).
Axes of the slice: x: 2, y: 2, z: 4, core: 2. Of those that a mesh axis runs over, the one named last changes fastest.
Arguments:
- matrix: bfloat16 [4, 1024, 2, 2048], P(None, 'prow', None, 'pcol'), may hold values from -6 to 6
- pivots: int32 [4, 256], replicated, may hold values from 0 to 4095, as said below
- lower_inverse: bfloat16 [4, 256, 256], replicated, as said below
- upper_inverse: bfloat16 [4, 256, 256], replicated, as said below
Outputs:
- factored: bfloat16 [4, 1024, 2, 2048], P(None, 'prow', None, 'pcol')
The draws below stay inside these ranges and needn't reach their ends.
Inputs may be any that keep to these rules, and one draw needn't show every extreme that they name: For step s and each i, pivots[s, i] is either s * 256 + i or a row index of s * 256 + 256 or more; the pivots of one step that differ from s * 256 + i are distinct. lower_inverse[s] is unit lower triangular. upper_inverse[s] is upper triangular.
All inputs are finite; a program needn't handle non-finite values.
Results may differ from the reference program's by a relative error of at most 0.0071.
Values may be sent and summed in bfloat16 or wider, within the bound.
No kernel may reach another device: no remote copies, remote signals or barrier semaphores. Data moves between devices by JAX's collectives and lax.ppermute only.
A program may use at most 64 MiB of HBM per device.

```python
import jax
import jax.numpy as jnp
from jax import lax

NB = 256
CB = 2
STEPS = 4
RB = 4
M = 4096
N_PROW = 4
N_PCOL = 8


def draw_pivots(key, part):
    stacked_rows = []
    for step_num in range(STEPS):
        step_key = jax.random.fold_in(key, step_num + 11)
        key_one, key_two = jax.random.split(step_key)
        lowest = (step_num + 1) * NB
        shuffled = jax.random.permutation(key_one, M - lowest).astype(jnp.int32)
        top_value = M - lowest - 1
        top_place = jnp.argmax(shuffled == top_value).astype(jnp.int32)
        second = shuffled[1]
        shuffled = shuffled.at[top_place].set(second).at[1].set(top_value)
        picked = lowest + shuffled[:NB]
        staying = jax.random.randint(key_two, (NB,), 0, 4) == 0
        staying = staying.at[1].set(False)
        if step_num == 0:
            staying = staying.at[0].set(True)
        own_rows = step_num * NB + jnp.arange(NB, dtype=jnp.int32)
        stacked_rows.append(jnp.where(staying, own_rows, picked.astype(jnp.int32)))
    return jnp.stack(stacked_rows).astype(jnp.int32)


def draw_upper_inverse(key, part):
    key_one, key_two = jax.random.split(jax.random.fold_in(key, 23))
    off_part = jax.random.normal(key_one, (STEPS, NB, NB), jnp.float32) / NB
    diag_part = jax.random.uniform(key_two, (STEPS, NB), jnp.float32, 0.5, 1.0)
    row_pos = lax.broadcasted_iota(jnp.int32, (NB, NB), 0)
    col_pos = lax.broadcasted_iota(jnp.int32, (NB, NB), 1)
    above = jnp.where(col_pos > row_pos, off_part, 0.0)
    on_diag = jnp.where(row_pos == col_pos, diag_part[:, :, None], 0.0) / NB ** 0.5
    return ((above + on_diag) * 0.25).astype(jnp.bfloat16)


def draw_lower_inverse(key, part):
    key_one = jax.random.fold_in(key, 37)
    off_part = jax.random.normal(key_one, (STEPS, NB, NB), jnp.float32) * 0.3 / NB ** 0.5
    row_pos = lax.broadcasted_iota(jnp.int32, (NB, NB), 0)
    col_pos = lax.broadcasted_iota(jnp.int32, (NB, NB), 1)
    below = jnp.where(row_pos > col_pos, off_part, 0.0)
    on_diag = jnp.where(row_pos == col_pos, 1.0, 0.0)
    return (below + on_diag).astype(jnp.bfloat16)


def block_levels(own_key, dims, pieces, least, high):
    def one(axis_at, blocks):
        draws = jax.random.uniform(jax.random.fold_in(jax.random.fold_in(own_key, 6), axis_at), (blocks,), jnp.float32, least / len(pieces), high / len(pieces))
        return jnp.repeat(jnp.exp(draws), dims[axis_at] // blocks).reshape((-1,) + (1,) * (len(dims) - axis_at - 1))

    factor_of = one(*pieces[0])
    for cut in pieces[1:]:
        factor_of = factor_of * one(*cut)
    return factor_of


def centred(stream_key, shape, width, limit, shards=(), kind=jnp.bfloat16):
    result = jax.random.normal(stream_key, shape, jnp.float32) * width
    if len(shards) > 0:
        result = block_levels(stream_key, shape, shards, -0.22, 0.18) * result
    return jnp.clip(result, min=-limit, max=limit).astype(kind)


def setup_inputs(seed: int = 0) -> dict:
    keys = jax.random.split(jax.random.key(seed), 5)
    return {
        "matrix": centred(keys[0], (RB, N_PROW * NB, CB, N_PCOL * NB), 1.0, 6.0, ((1, 4), (3, 8))),
        "pivots": draw_pivots(jax.random.fold_in(keys[4], 71), 0),
        "lower_inverse": draw_lower_inverse(jax.random.fold_in(keys[4], 71), 0),
        "upper_inverse": draw_upper_inverse(jax.random.fold_in(keys[4], 71), 0),
    }


def reference(matrix, pivots, lower_inverse, upper_inverse):
    whole = matrix.reshape(M, M)
    for step_num in range(STEPS):
        begin_at = step_num * NB
        trail_at = begin_at + NB
        targets = begin_at + jnp.arange(NB, dtype=jnp.int32)
        chosen = pivots[step_num].astype(jnp.int32)
        order_map = jnp.arange(M, dtype=jnp.int32).at[chosen].set(targets).at[targets].set(chosen)
        whole = whole[order_map]
        left_block = jnp.dot(whole[trail_at:, begin_at:trail_at], upper_inverse[step_num], preferred_element_type=jnp.float32).astype(jnp.bfloat16)
        upper_block = jnp.dot(lower_inverse[step_num], whole[begin_at:trail_at, trail_at:], preferred_element_type=jnp.float32).astype(jnp.bfloat16)
        corner = (whole[trail_at:, trail_at:].astype(jnp.float32) - jnp.dot(left_block, upper_block, preferred_element_type=jnp.float32)).astype(jnp.bfloat16)
        whole = whole.at[trail_at:, begin_at:trail_at].set(left_block)
        whole = whole.at[begin_at:trail_at, trail_at:].set(upper_block)
        whole = whole.at[trail_at:, trail_at:].set(corner)
    return whole.reshape(matrix.shape)
```

```python
import functools

import jax
import jax.numpy as jnp
from jax import lax
from jax.experimental import pallas as pl
from jax.experimental.pallas import tpu as pltpu
from jax.sharding import PartitionSpec as P

BF16 = jnp.bfloat16
F32 = jnp.float32
I32 = jnp.int32
VMEM_BYTES = 44 * 1024 * 1024
MOVE_ROWS = 96
MOVE_SLOTS = 128


def spread(value, axis, source):
    kept = jnp.where(lax.axis_index(axis) == source, value, 0).astype(value.dtype)
    return lax.psum(kept, axis)


def stepwise(matrix, pivots, lower_inverse, upper_inverse):
    row_blocks = matrix.shape[0]
    block_size = matrix.shape[1]
    col_blocks = matrix.shape[2]
    local_rows = row_blocks * block_size
    local_cols = col_blocks * block_size
    matrix_loc = matrix.reshape(local_rows, local_cols)
    row_count = lax.axis_size("prow")
    col_count = lax.axis_size("pcol")
    my_row = lax.axis_index("prow")
    my_col = lax.axis_index("pcol")
    row_iota = jnp.arange(local_rows, dtype=jnp.int32)
    col_iota = jnp.arange(local_cols, dtype=jnp.int32)
    global_row = (row_iota // block_size * row_count + my_row) * block_size + row_iota % block_size
    global_col = (col_iota // block_size * col_count + my_col) * block_size + col_iota % block_size
    for step_num in range(pivots.shape[0]):
        begin_at = step_num * block_size
        trail_at = begin_at + block_size
        diag_root = step_num % row_count
        diag_local = step_num // row_count * block_size
        panel_root = step_num % col_count
        panel_local = step_num // col_count * block_size
        targets = begin_at + jnp.arange(block_size, dtype=jnp.int32)
        chosen = pivots[step_num]
        chosen_block = chosen // block_size
        chosen_owner = chosen_block % row_count
        is_mine = chosen_owner == my_row
        chosen_local = chosen_block // row_count * block_size + chosen % block_size
        picked = jnp.take(matrix_loc, jnp.where(is_mine, chosen_local, 0), axis=0)
        picked = jnp.where(is_mine[:, None], picked, jnp.zeros_like(picked))
        diag_rows = matrix_loc[diag_local : diag_local + block_size]
        own_diag = jnp.where(my_row == diag_root, diag_rows, jnp.zeros_like(diag_rows))
        new_rows, old_diag = lax.psum(picked, "prow"), lax.psum(own_diag, "prow")
        moved_rows = is_mine & (chosen != targets)
        matrix_loc = matrix_loc.at[jnp.where(moved_rows, chosen_local, local_rows)].set(
            old_diag, mode="drop"
        )
        diag_after = matrix_loc[diag_local : diag_local + block_size]
        matrix_loc = matrix_loc.at[diag_local : diag_local + block_size].set(
            jnp.where(my_row == diag_root, new_rows, diag_after)
        )
        upper_full = jnp.dot(
            lower_inverse[step_num], new_rows, preferred_element_type=jnp.float32
        ).astype(jnp.bfloat16)
        col_live = global_col >= trail_at
        upper_use = jnp.where(col_live[None, :], upper_full, jnp.zeros_like(upper_full))
        panel_own = matrix_loc[:, panel_local : panel_local + block_size]
        received = spread(panel_own, "pcol", panel_root)
        left_full = jnp.dot(
            received, upper_inverse[step_num], preferred_element_type=jnp.float32
        ).astype(jnp.bfloat16)
        row_live = global_row >= trail_at
        left_use = jnp.where(row_live[:, None], left_full, jnp.zeros_like(left_full))
        matrix_loc = (
            matrix_loc.astype(jnp.float32)
            - jnp.dot(left_use, upper_use, preferred_element_type=jnp.float32)
        ).astype(jnp.bfloat16)
        panel_now = matrix_loc[:, panel_local : panel_local + block_size]
        panel_put = jnp.where(row_live[:, None] & (my_col == panel_root), left_full, panel_now)
        matrix_loc = matrix_loc.at[:, panel_local : panel_local + block_size].set(panel_put)
        diag_now = matrix_loc[diag_local : diag_local + block_size]
        diag_put = jnp.where(col_live[None, :] & (my_row == diag_root), upper_full, diag_now)
        matrix_loc = matrix_loc.at[diag_local : diag_local + block_size].set(diag_put)
    return matrix_loc.reshape(matrix.shape)


def iota(shape, dim):
    return lax.broadcasted_iota(I32, shape, dim)


def dot(a, b):
    return jnp.dot(a, b, preferred_element_type=F32)


def one_hot(hit):
    return jnp.where(hit, 1.0, 0.0).astype(BF16)


def to_col(row, size):
    eye = iota((size, size), 0) == iota((size, size), 1)
    return jnp.sum(jnp.where(eye, jnp.broadcast_to(row, (size, size)), 0), axis=1, keepdims=True)


def find(col, base, x, size):
    hit = col == x
    place = jnp.sum(jnp.where(hit, iota((size, size), 0) + (base + 1), 0), axis=0, keepdims=True)
    return jnp.where(place > 0, place - 1, x)


def look(col, base, x, size):
    hit = iota((size, size), 0) + base == x
    return jnp.sum(jnp.where(hit, col, 0), axis=0, keepdims=True)


def before(rows, size):
    tri = one_hot(iota((size, size), 0) < iota((size, size), 1))
    stacked = jnp.concatenate([one_hot(r) for r in rows], axis=0)
    counts = dot(stacked, tri)
    k = rows[0].shape[0]
    return [counts[i * k : (i + 1) * k] for i in range(len(rows))]


def pick_kernel(cfg, piv_ref, m0_ref, m1_ref, meta_ref, pack0_ref, pack1_ref):
    nb, steps, n_row, cap, local_rows = cfg
    my_row = lax.axis_index("prow")
    piv = [piv_ref[t : t + 1, :] for t in range(steps)]
    cols = [to_col(piv[t], nb) for t in range(steps - 1)]
    owners, places = [], []
    for t in range(steps):
        x = piv[t]
        for s in range(t - 1, -1, -1):
            x = find(cols[s], s * nb, x, nb)
        block = x // nb
        owners.append(block % n_row)
        places.append(block // n_row * nb + x % nb)
    lanes = -(-n_row // 8) * 8
    member = [iota((lanes, nb), 0) == w for w in owners]
    counts = before(member, nb)
    base = jnp.zeros((lanes, 1), F32)
    ranks = []
    for t in range(steps):
        ranks.append(
            jnp.sum(jnp.where(member[t], counts[t] + base, 0.0), axis=0, keepdims=True).astype(I32)
        )
        base = base + jnp.sum(jnp.where(member[t], 1.0, 0.0), axis=1, keepdims=True)
    for t in range(steps):
        meta_ref[t : t + 1, :] = owners[t] * cap + ranks[t]
    over = jnp.max(base, axis=0, keepdims=True).astype(I32)
    meta_ref[steps : steps + 1, :] = jnp.broadcast_to(over, (1, nb))
    slot = iota((cap, nb), 0)
    total = jnp.zeros((cap, nb), I32)
    for t in range(steps):
        key = jnp.where(owners[t] == my_row, ranks[t], -1)
        total = total + jnp.where(slot == key, places[t] + 1, 0)
    source = jnp.sum(total, axis=1, keepdims=True) - 1
    chosen = one_hot(source == iota((cap, local_rows), 1))
    pack0_ref[...] = dot(chosen, m0_ref[...]).astype(BF16)
    pack1_ref[...] = dot(chosen, m1_ref[...]).astype(BF16)


def move_kernel(cfg, piv_ref, meta_ref, move_ref):
    nb, steps, n_row, cap = cfg
    piv = [piv_ref[t : t + 1, :] for t in range(steps)]
    cols = [to_col(piv[t], nb) for t in range(steps)]
    lanes = -(-n_row // 8) * 8
    dests, member = [], []
    for t in range(steps):
        at = iota((1, nb), 1) + t * nb
        x = at
        for s in range(t):
            x = find(cols[s], s * nb, x, nb)
        x = jnp.where(x == at, piv[t], x)
        for s in range(t + 1, steps):
            inside = (x >= s * nb) & (x < (s + 1) * nb)
            x = jnp.where(inside, look(cols[s], s * nb, x, nb), find(cols[s], s * nb, x, nb))
        block = x // nb
        dest = jnp.where(x >= steps * nb, block % n_row, -1)
        move_ref[t : t + 1, :] = dest
        move_ref[2 * steps + t : 2 * steps + t + 1, :] = block // n_row * nb + x % nb
        member.append(iota((lanes, nb), 0) == dest)
    counts = before(member, nb)
    most = jnp.zeros((lanes, 1), F32)
    for t in range(steps):
        move_ref[steps + t : steps + t + 1, :] = jnp.sum(
            jnp.where(member[t], counts[t], 0.0), axis=0, keepdims=True
        ).astype(I32)
        most = jnp.maximum(most, jnp.sum(jnp.where(member[t], 1.0, 0.0), axis=1, keepdims=True))
    over = jnp.max(most, axis=0, keepdims=True).astype(I32)
    bad = (over > MOVE_ROWS) | (meta_ref[steps : steps + 1, :] > cap)
    move_ref[3 * steps : 3 * steps + 1, :] = jnp.where(bad, 1, 0)


def order_rows(meta_ref, buf_ref, t, nb):
    pos = to_col(meta_ref[t : t + 1, :], nb)
    hot = one_hot(pos == iota((nb, buf_ref.shape[0]), 1))
    return dot(hot, buf_ref[...]).astype(BF16)


def order_kernel(cfg, meta_ref, buf_ref, top_ref, off_ref):
    nb, steps = cfg
    my_col = lax.axis_index("pcol")
    for t in range(steps):
        top_ref[t * nb : (t + 1) * nb, :] = order_rows(meta_ref, buf_ref, t, nb)
    for j in range(steps - 1):
        block = jnp.where(my_col <= j, j + 1, j)
        rows = pl.ds(pl.multiple_of(block * nb, nb), nb)
        off_ref[j * nb : (j + 1) * nb, :] = top_ref[rows, :]


def factor_kernel(
    cfg, meta_ref, move_ref, top0_ref, buf1_ref, m0_ref, m1_ref, raw_a, raw_b, off_a, off_b,
    linv_ref, uinv_ref, res_ref, top_ref, send_ref, raw, off, l_own, l_top, u_top, upper, first,
    diag, sems,
):
    nb, steps, n_row, local_rows = cfg
    my_row = lax.axis_index("prow")
    my_col = lax.axis_index("pcol")
    low = my_col & 3
    copies = []
    for i, (src, at, mask) in enumerate(
        [(off_a, 0, 0), (off_a, 1, 2), (off_b, 0, 1), (off_b, 1, 3)]
    ):
        copies.append(pltpu.make_async_copy(src.at[at], off.at[low ^ mask], sems.at[i]))
    for i, (src, at, mask) in enumerate(
        [(raw_a, 0, 0), (raw_a, 1, 2), (raw_b, 0, 1), (raw_b, 1, 3)]
    ):
        copies.append(pltpu.make_async_copy(src.at[at], raw.at[low ^ mask], sems.at[4 + i]))
    for c in copies:
        c.start()
    wide = steps * nb
    for t in range(steps):
        first[t * nb : (t + 1) * nb, :nb] = top0_ref[t * nb : (t + 1) * nb, :]
        first[t * nb : (t + 1) * nb, nb:] = order_rows(meta_ref, buf1_ref, t, nb)
    for c in copies:
        c.wait()
    for t in range(steps):
        here = slice(t * nb, (t + 1) * nb)
        done = slice(0, t * nb)
        for s in range(t):
            sel = slice(s * nb, (s + 1) * nb)
            acc = off[t, sel, :].astype(F32)
            if s > 0:
                acc = acc - dot(l_top[sel, : s * nb], u_top[: s * nb, here])
            u_top[sel, here] = dot(linv_ref[s], acc.astype(BF16)).astype(BF16)
        if t < steps - 1:
            acc = off[t, t * nb :, :].astype(F32)
            if t > 0:
                acc = acc - dot(l_top[(t + 1) * nb :, done], u_top[done, here])
            l_top[(t + 1) * nb :, here] = dot(acc.astype(BF16), uinv_ref[t]).astype(BF16)
        for k in range(local_rows // nb):
            rows = slice(k * nb, (k + 1) * nb)
            acc = raw[t, rows, :].astype(F32)
            if t > 0:
                acc = acc - dot(l_own[rows, done], u_top[done, here])
            l_own[rows, here] = dot(acc.astype(BF16), uinv_ref[t]).astype(BF16)
        acc = first[here, :].astype(F32)
        if t > 0:
            acc = acc - dot(l_top[here, done], upper[done, :])
        acc = acc.astype(BF16)
        diag[here, :] = acc[:, :nb]
        upper[here, :] = dot(linv_ref[t], acc).astype(BF16)
    in_panel = my_col < steps
    panel = pl.ds(pl.multiple_of(jnp.minimum(my_col, steps - 1) * nb, nb), nb)
    for k in range(local_rows // nb):
        rows = slice(k * nb, (k + 1) * nb)
        prod = dot(l_own[rows, :], upper[...])
        left = (m0_ref[rows, :].astype(F32) - prod[:, :nb]).astype(BF16)
        res_ref[rows, :nb] = jnp.where(in_panel, l_own[rows, panel], left)
        res_ref[rows, nb:] = (m1_ref[rows, :].astype(F32) - prod[:, nb:]).astype(BF16)
    block = pl.ds(pl.multiple_of(jnp.minimum(my_row, steps - 1) * nb, nb), nb)
    own_upper = upper[block, :]
    left = jnp.where(my_col == my_row, diag[block, :], own_upper[:, :nb])
    left = jnp.where(in_panel & (my_col < my_row), l_top[block, panel], left)
    top_ref[:, :nb] = left
    top_ref[:, nb:] = own_upper[:, nb:]
    here = iota((steps, nb), 0) == my_row
    dest = jnp.sum(jnp.where(here, move_ref[:steps, :] + 1, 0), axis=0, keepdims=True) - 1
    rank = jnp.sum(jnp.where(here, move_ref[steps : 2 * steps, :], 0), axis=0, keepdims=True)
    for k in range(n_row):
        key = jnp.where(dest == lax.rem(my_row + k, n_row), rank, -1)
        hot = one_hot(key == iota((MOVE_ROWS, nb), 0))
        send_ref[k] = dot(hot, res_ref[:nb, :]).astype(BF16)


def place_kernel(cfg, move_ref, res_ref, top_ref, *refs):
    nb, steps, n_row, local_rows = cfg
    recv, out_ref, slots = refs[:n_row], refs[n_row], refs[n_row + 1]
    my_row = lax.axis_index("prow")
    slots[...] = jnp.zeros_like(slots)
    targets = []
    for k in range(n_row):
        slots[k * MOVE_SLOTS : k * MOVE_SLOTS + MOVE_ROWS, :] = recv[k][...]
        source = lax.rem(my_row + n_row - k, n_row)
        here = iota((steps, nb), 0) == source
        dest = jnp.sum(jnp.where(here, move_ref[:steps, :] + 1, 0), axis=0, keepdims=True) - 1
        rank = jnp.sum(jnp.where(here, move_ref[steps : 2 * steps, :], 0), axis=0, keepdims=True)
        place = jnp.sum(
            jnp.where(here, move_ref[2 * steps : 3 * steps, :], 0), axis=0, keepdims=True
        )
        key = jnp.where(dest == my_row, rank, -1)
        hot = one_hot(key == iota((MOVE_SLOTS, nb), 0))
        row = iota((8, nb), 0)
        parts = jnp.where(row == 0, place // 128, jnp.where(row == 1, place % 128, 1))
        found = lax.dot_general(
            parts.astype(F32).astype(BF16), hot, (((1,), (1,)), ((), ())),
            preferred_element_type=F32,
        )
        at = found[0:1] * 128.0 + found[1:2]
        targets.append(jnp.where(found[2:3] > 0.5, at, -1.0).astype(I32))
    target = jnp.concatenate(targets, axis=1)
    for k in range(local_rows // nb):
        rows = slice(k * nb, (k + 1) * nb)
        hit = iota((nb, n_row * MOVE_SLOTS), 0) + k * nb == target
        moved = dot(one_hot(hit), slots[...]).astype(BF16)
        any_hit = jnp.sum(jnp.where(hit, 1.0, 0.0), axis=1, keepdims=True) > 0.5
        value = jnp.where(any_hit, moved, res_ref[rows, :])
        if k == 0:
            value = jnp.where(my_row < steps, top_ref[...], value)
        out_ref[rows, :] = value


def call(kernel, outs, ins, scratch=(), any_at=()):
    vmem = pl.BlockSpec(memory_space=pltpu.VMEM)
    anywhere = pl.BlockSpec(memory_space=pl.ANY)
    return pl.pallas_call(
        kernel,
        out_shape=outs,
        in_specs=[anywhere if i in any_at else vmem for i in range(len(ins))],
        out_specs=jax.tree.map(lambda _: vmem, outs),
        scratch_shapes=list(scratch),
        compiler_params=pltpu.CompilerParams(vmem_limit_bytes=VMEM_BYTES),
    )(*ins)


def shape(*dims, dtype=BF16):
    return jax.ShapeDtypeStruct(dims, dtype)


def local(matrix, pivots, lower_inverse, upper_inverse):
    row_blocks, nb, col_blocks, _ = matrix.shape
    steps = pivots.shape[0]
    n_row = lax.axis_size("prow")
    n_col = lax.axis_size("pcol")
    if steps != 4 or col_blocks != 2 or n_row < steps or n_col < 8 or n_col % 4:
        return stepwise(matrix, pivots, lower_inverse, upper_inverse)
    my_col = lax.axis_index("pcol")
    local_rows = row_blocks * nb
    cap = -(-(steps * nb // n_row + 64) // 16) * 16
    m0 = matrix[:, :, 0, :].reshape(local_rows, nb)
    m1 = matrix[:, :, 1, :].reshape(local_rows, nb)

    def from_panels(value, mask):
        return lax.ppermute(value, "pcol", [(i, i ^ mask) for i in range(steps)])

    def swap_cores(value):
        return lax.ppermute(value, "pcol", [(i, i ^ 1) for i in range(n_col)])

    on_panel = my_col < steps
    fours = range(4, n_col, 4)
    raw_x = from_panels(m0, 2)
    raw_far = functools.reduce(jnp.add, [from_panels(m0, mask) for mask in fours])

    meta, pack0, pack1 = call(
        functools.partial(pick_kernel, (nb, steps, n_row, cap, local_rows)),
        (shape(8, nb, dtype=I32), shape(cap, nb), shape(cap, nb)),
        (pivots, m0, m1),
    )
    buf0 = lax.all_gather(pack0, "prow", tiled=True)
    top0, off = call(
        functools.partial(order_kernel, (nb, steps)),
        (shape(steps * nb, nb), shape((steps - 1) * nb, nb)),
        (meta, buf0),
    )
    raw_far_x = lax.ppermute(raw_far, "pcol", [(i, i ^ 2) for i in range(steps, n_col)])
    off_x = from_panels(off, 2)
    off_far = functools.reduce(jnp.add, [from_panels(off, mask) for mask in fours])
    off_far_x = functools.reduce(jnp.add, [from_panels(off, mask + 2) for mask in fours])
    pack1, _ = lax.optimization_barrier((pack1, off))
    buf1 = lax.all_gather(pack1, "prow", tiled=True)
    move = call(
        functools.partial(move_kernel, (nb, steps, n_row, cap)),
        shape(16, nb, dtype=I32),
        (pivots, meta),
    )
    raw_a = jnp.stack([jnp.where(on_panel, m0, raw_far), jnp.where(on_panel, raw_x, raw_far_x)])
    raw_b = swap_cores(raw_a)
    off_a = jnp.stack([jnp.where(on_panel, off, off_far), jnp.where(on_panel, off_x, off_far_x)])
    off_b = swap_cores(off_a)
    top_rows = steps * nb
    res, top, send = call(
        functools.partial(factor_kernel, (nb, steps, n_row, local_rows)),
        (shape(local_rows, 2 * nb), shape(nb, 2 * nb), shape(n_row, MOVE_ROWS, 2 * nb)),
        (meta, move, top0, buf1, m0, m1, raw_a, raw_b, off_a, off_b, lower_inverse, upper_inverse),
        scratch=(
            pltpu.VMEM((steps, local_rows, nb), BF16),
            pltpu.VMEM((steps, top_rows - nb, nb), BF16),
            pltpu.VMEM((local_rows, top_rows), BF16),
            pltpu.VMEM((top_rows, top_rows), BF16),
            pltpu.VMEM((top_rows, top_rows), BF16),
            pltpu.VMEM((top_rows, 2 * nb), BF16),
            pltpu.VMEM((top_rows, 2 * nb), BF16),
            pltpu.VMEM((top_rows, nb), BF16),
            pltpu.SemaphoreType.DMA((8,)),
        ),
        any_at=(6, 7, 8, 9),
    )
    recv = [send[0]] + [
        lax.ppermute(send[k], "prow", [(i, (i + k) % n_row) for i in range(n_row)])
        for k in range(1, n_row)
    ]

    def finish():
        out = call(
            functools.partial(place_kernel, (nb, steps, n_row, local_rows)),
            shape(local_rows, 2 * nb),
            (move, res, top, *recv),
            scratch=(pltpu.VMEM((n_row * MOVE_SLOTS, 2 * nb), BF16),),
        )
        return out.reshape(matrix.shape)

    return lax.cond(
        move[3 * steps, 0] > 0,
        lambda: stepwise(matrix, pivots, lower_inverse, upper_inverse),
        finish,
    )


def solution(mesh):
    placed = (P(None, "prow", None, "pcol"), P(), P(), P())
    return jax.shard_map(
        local, mesh=mesh, in_specs=placed, out_specs=P(None, "prow", None, "pcol"), check_vma=False
    )
```

```python
import functools

import jax
import jax.numpy as jnp
from jax import lax
from jax.experimental import pallas as pl
from jax.experimental.pallas import tpu as pltpu
from jax.sharding import PartitionSpec as P

BF16 = jnp.bfloat16
F32 = jnp.float32
I32 = jnp.int32
VMEM_BYTES = 44 * 1024 * 1024
MOVE_ROWS = 96
MOVE_SLOTS = 128


def ring_sum(value, axis):
    size = lax.axis_size(axis)

    def turn(_, carry):
        total, passing = carry
        passing = lax.ppermute(passing, axis, [(i, (i + 1) % size) for i in range(size)])
        return total + passing, passing

    return lax.fori_loop(1, size, turn, (value, value))[0]


def spread(value, axis, source):
    kept = jnp.where(lax.axis_index(axis) == source, value, 0).astype(value.dtype)
    return ring_sum(kept, axis)


def stepwise(matrix, pivots, lower_inverse, upper_inverse):
    row_blocks = matrix.shape[0]
    block_size = matrix.shape[1]
    col_blocks = matrix.shape[2]
    local_rows = row_blocks * block_size
    local_cols = col_blocks * block_size
    matrix_loc = matrix.reshape(local_rows, local_cols)
    row_count = lax.axis_size("prow")
    col_count = lax.axis_size("pcol")
    my_row = lax.axis_index("prow")
    my_col = lax.axis_index("pcol")
    row_iota = jnp.arange(local_rows, dtype=jnp.int32)
    col_iota = jnp.arange(local_cols, dtype=jnp.int32)
    global_row = (row_iota // block_size * row_count + my_row) * block_size + row_iota % block_size
    global_col = (col_iota // block_size * col_count + my_col) * block_size + col_iota % block_size
    for step_num in range(pivots.shape[0]):
        begin_at = step_num * block_size
        trail_at = begin_at + block_size
        diag_root = step_num % row_count
        diag_local = step_num // row_count * block_size
        panel_root = step_num % col_count
        panel_local = step_num // col_count * block_size
        targets = begin_at + jnp.arange(block_size, dtype=jnp.int32)
        chosen = pivots[step_num]
        chosen_block = chosen // block_size
        chosen_owner = chosen_block % row_count
        is_mine = chosen_owner == my_row
        chosen_local = chosen_block // row_count * block_size + chosen % block_size
        picked = jnp.take(matrix_loc, jnp.where(is_mine, chosen_local, 0), axis=0)
        picked = jnp.where(is_mine[:, None], picked, jnp.zeros_like(picked))
        diag_rows = matrix_loc[diag_local : diag_local + block_size]
        own_diag = jnp.where(my_row == diag_root, diag_rows, jnp.zeros_like(diag_rows))
        new_rows, old_diag = ring_sum(picked, "prow"), ring_sum(own_diag, "prow")
        moved_rows = is_mine & (chosen != targets)
        matrix_loc = matrix_loc.at[jnp.where(moved_rows, chosen_local, local_rows)].set(
            old_diag, mode="drop"
        )
        diag_after = matrix_loc[diag_local : diag_local + block_size]
        matrix_loc = matrix_loc.at[diag_local : diag_local + block_size].set(
            jnp.where(my_row == diag_root, new_rows, diag_after)
        )
        upper_full = jnp.dot(
            lower_inverse[step_num], new_rows, preferred_element_type=jnp.float32
        ).astype(jnp.bfloat16)
        col_live = global_col >= trail_at
        upper_use = jnp.where(col_live[None, :], upper_full, jnp.zeros_like(upper_full))
        panel_own = matrix_loc[:, panel_local : panel_local + block_size]
        received = spread(panel_own, "pcol", panel_root)
        left_full = jnp.dot(
            received, upper_inverse[step_num], preferred_element_type=jnp.float32
        ).astype(jnp.bfloat16)
        row_live = global_row >= trail_at
        left_use = jnp.where(row_live[:, None], left_full, jnp.zeros_like(left_full))
        matrix_loc = (
            matrix_loc.astype(jnp.float32)
            - jnp.dot(left_use, upper_use, preferred_element_type=jnp.float32)
        ).astype(jnp.bfloat16)
        panel_now = matrix_loc[:, panel_local : panel_local + block_size]
        panel_put = jnp.where(row_live[:, None] & (my_col == panel_root), left_full, panel_now)
        matrix_loc = matrix_loc.at[:, panel_local : panel_local + block_size].set(panel_put)
        diag_now = matrix_loc[diag_local : diag_local + block_size]
        diag_put = jnp.where(col_live[None, :] & (my_row == diag_root), upper_full, diag_now)
        matrix_loc = matrix_loc.at[diag_local : diag_local + block_size].set(diag_put)
    return matrix_loc.reshape(matrix.shape)


def iota(shape, dim):
    return lax.broadcasted_iota(I32, shape, dim)


def dot(a, b):
    return jnp.dot(a, b, preferred_element_type=F32)


def one_hot(hit):
    return jnp.where(hit, 1.0, 0.0).astype(BF16)


def to_col(row, size):
    eye = iota((size, size), 0) == iota((size, size), 1)
    return jnp.sum(jnp.where(eye, jnp.broadcast_to(row, (size, size)), 0), axis=1, keepdims=True)


def find(col, base, x, size):
    hit = col == x
    place = jnp.sum(jnp.where(hit, iota((size, size), 0) + (base + 1), 0), axis=0, keepdims=True)
    return jnp.where(place > 0, place - 1, x)


def look(col, base, x, size):
    hit = iota((size, size), 0) + base == x
    return jnp.sum(jnp.where(hit, col, 0), axis=0, keepdims=True)


def before(rows, size):
    tri = one_hot(iota((size, size), 0) < iota((size, size), 1))
    stacked = jnp.concatenate([one_hot(r) for r in rows], axis=0)
    counts = dot(stacked, tri)
    k = rows[0].shape[0]
    return [counts[i * k : (i + 1) * k] for i in range(len(rows))]


def pick_kernel(cfg, piv_ref, mat_ref, meta_ref, pack0_ref, pack1_ref):
    nb, steps, n_row, cap, local_rows = cfg
    my_row = lax.axis_index("prow")
    piv = [piv_ref[t : t + 1, :] for t in range(steps)]
    cols = [to_col(piv[t], nb) for t in range(steps - 1)]
    owners, places = [], []
    for t in range(steps):
        x = piv[t]
        for s in range(t - 1, -1, -1):
            x = find(cols[s], s * nb, x, nb)
        block = x // nb
        owners.append(block % n_row)
        places.append(block // n_row * nb + x % nb)
    lanes = -(-n_row // 8) * 8
    member = [iota((lanes, nb), 0) == w for w in owners]
    counts = before(member, nb)
    base = jnp.zeros((lanes, 1), F32)
    ranks = []
    for t in range(steps):
        ranks.append(
            jnp.sum(jnp.where(member[t], counts[t] + base, 0.0), axis=0, keepdims=True).astype(I32)
        )
        base = base + jnp.sum(jnp.where(member[t], 1.0, 0.0), axis=1, keepdims=True)
    for t in range(steps):
        meta_ref[t : t + 1, :] = owners[t] * cap + ranks[t]
    over = jnp.max(base, axis=0, keepdims=True).astype(I32)
    meta_ref[steps : steps + 1, :] = jnp.broadcast_to(over, (1, nb))
    slot = iota((cap, nb), 0)
    total = jnp.zeros((cap, nb), I32)
    for t in range(steps):
        key = jnp.where(owners[t] == my_row, ranks[t], -1)
        total = total + jnp.where(slot == key, places[t] + 1, 0)
    source = jnp.sum(total, axis=1, keepdims=True) - 1
    chosen = one_hot(source == iota((cap, local_rows), 1))
    pack0_ref[...] = dot(chosen, mat_ref[0]).astype(BF16)
    pack1_ref[...] = dot(chosen, mat_ref[1]).astype(BF16)


def move_kernel(cfg, piv_ref, meta_ref, move_ref):
    nb, steps, n_row, cap = cfg
    piv = [piv_ref[t : t + 1, :] for t in range(steps)]
    cols = [to_col(piv[t], nb) for t in range(steps)]
    lanes = -(-n_row // 8) * 8
    dests, member = [], []
    for t in range(steps):
        at = iota((1, nb), 1) + t * nb
        x = at
        for s in range(t):
            x = find(cols[s], s * nb, x, nb)
        x = jnp.where(x == at, piv[t], x)
        for s in range(t + 1, steps):
            inside = (x >= s * nb) & (x < (s + 1) * nb)
            x = jnp.where(inside, look(cols[s], s * nb, x, nb), find(cols[s], s * nb, x, nb))
        block = x // nb
        dest = jnp.where(x >= steps * nb, block % n_row, -1)
        move_ref[t : t + 1, :] = dest
        move_ref[2 * steps + t : 2 * steps + t + 1, :] = block // n_row * nb + x % nb
        member.append(iota((lanes, nb), 0) == dest)
    counts = before(member, nb)
    most = jnp.zeros((lanes, 1), F32)
    for t in range(steps):
        move_ref[steps + t : steps + t + 1, :] = jnp.sum(
            jnp.where(member[t], counts[t], 0.0), axis=0, keepdims=True
        ).astype(I32)
        most = jnp.maximum(most, jnp.sum(jnp.where(member[t], 1.0, 0.0), axis=1, keepdims=True))
    over = jnp.max(most, axis=0, keepdims=True).astype(I32)
    bad = (over > MOVE_ROWS) | (meta_ref[steps : steps + 1, :] > cap)
    move_ref[3 * steps : 3 * steps + 1, :] = jnp.where(bad, 1, 0)


def order_rows(meta_ref, buf_ref, t, nb):
    pos = to_col(meta_ref[t : t + 1, :], nb)
    hot = one_hot(pos == iota((nb, buf_ref.shape[0]), 1))
    return dot(hot, buf_ref[...]).astype(BF16)


def order_kernel(cfg, meta_ref, buf_ref, top_ref, off_ref):
    nb, steps = cfg
    my_col = lax.axis_index("pcol")
    for t in range(steps):
        top_ref[t * nb : (t + 1) * nb, :] = order_rows(meta_ref, buf_ref, t, nb)
    for j in range(steps - 1):
        block = jnp.where(my_col <= j, j + 1, j)
        rows = pl.ds(pl.multiple_of(block * nb, nb), nb)
        off_ref[j * nb : (j + 1) * nb, :] = top_ref[rows, :]


def factor_kernel(
    cfg, meta_ref, move_ref, top0_ref, buf1_ref, mat_ref, raw_0, raw_2, raw_1, raw_3,
    off_0, off_2, off_1, off_3, linv_ref, uinv_ref, res_ref, top_ref, send_ref, raw, off, l_own, l_top, u_top, upper, first,
    diag, sems,
):
    nb, steps, n_row, local_rows = cfg
    my_row = lax.axis_index("prow")
    my_col = lax.axis_index("pcol")
    low = my_col & 3
    copies = [
        pltpu.make_async_copy(src, dst.at[low ^ mask], sems.at[i])
        for i, (src, dst, mask) in enumerate(
            [(off_0, off, 0), (off_1, off, 1), (off_2, off, 2), (off_3, off, 3)]
            + [(raw_0, raw, 0), (raw_1, raw, 1), (raw_2, raw, 2), (raw_3, raw, 3)]
        )
    ]
    for c in copies:
        c.start()
    wide = steps * nb
    for t in range(steps):
        first[t * nb : (t + 1) * nb, :nb] = top0_ref[t * nb : (t + 1) * nb, :]
        first[t * nb : (t + 1) * nb, nb:] = order_rows(meta_ref, buf1_ref, t, nb)
    for c in copies:
        c.wait()
    for t in range(steps):
        here = slice(t * nb, (t + 1) * nb)
        done = slice(0, t * nb)
        for s in range(t):
            sel = slice(s * nb, (s + 1) * nb)
            acc = off[t, sel, :].astype(F32)
            if s > 0:
                acc = acc - dot(l_top[sel, : s * nb], u_top[: s * nb, here])
            u_top[sel, here] = dot(linv_ref[s], acc.astype(BF16)).astype(BF16)
        if t < steps - 1:
            acc = off[t, t * nb :, :].astype(F32)
            if t > 0:
                acc = acc - dot(l_top[(t + 1) * nb :, done], u_top[done, here])
            l_top[(t + 1) * nb :, here] = dot(acc.astype(BF16), uinv_ref[t]).astype(BF16)
        for k in range(local_rows // nb):
            rows = slice(k * nb, (k + 1) * nb)
            acc = raw[t, rows, :].astype(F32)
            if t > 0:
                acc = acc - dot(l_own[rows, done], u_top[done, here])
            l_own[rows, here] = dot(acc.astype(BF16), uinv_ref[t]).astype(BF16)
        acc = first[here, :].astype(F32)
        if t > 0:
            acc = acc - dot(l_top[here, done], upper[done, :])
        acc = acc.astype(BF16)
        diag[here, :] = acc[:, :nb]
        upper[here, :] = dot(linv_ref[t], acc).astype(BF16)
    in_panel = my_col < steps
    panel = pl.ds(pl.multiple_of(jnp.minimum(my_col, steps - 1) * nb, nb), nb)
    for k in range(local_rows // nb):
        rows = slice(k * nb, (k + 1) * nb)
        prod = dot(l_own[rows, :], upper[...])
        left = (mat_ref[0, rows, :].astype(F32) - prod[:, :nb]).astype(BF16)
        res_ref[rows, :nb] = jnp.where(in_panel, l_own[rows, panel], left)
        res_ref[rows, nb:] = (mat_ref[1, rows, :].astype(F32) - prod[:, nb:]).astype(BF16)
    block = pl.ds(pl.multiple_of(jnp.minimum(my_row, steps - 1) * nb, nb), nb)
    own_upper = upper[block, :]
    left = jnp.where(my_col == my_row, diag[block, :], own_upper[:, :nb])
    left = jnp.where(in_panel & (my_col < my_row), l_top[block, panel], left)
    top_ref[:, :nb] = left
    top_ref[:, nb:] = own_upper[:, nb:]
    here = iota((steps, nb), 0) == my_row
    dest = jnp.sum(jnp.where(here, move_ref[:steps, :] + 1, 0), axis=0, keepdims=True) - 1
    rank = jnp.sum(jnp.where(here, move_ref[steps : 2 * steps, :], 0), axis=0, keepdims=True)
    for k in range(n_row):
        key = jnp.where(dest == lax.rem(my_row + k, n_row), rank, -1)
        hot = one_hot(key == iota((MOVE_ROWS, nb), 0))
        send_ref[k] = dot(hot, res_ref[:nb, :]).astype(BF16)


def place_kernel(cfg, move_ref, res_ref, top_ref, *refs):
    nb, steps, n_row, local_rows = cfg
    recv, out_ref, slots = refs[:n_row], refs[n_row], refs[n_row + 1]
    my_row = lax.axis_index("prow")
    slots[...] = jnp.zeros_like(slots)
    targets = []
    for k in range(n_row):
        slots[k * MOVE_SLOTS : k * MOVE_SLOTS + MOVE_ROWS, :] = recv[k][...]
        source = lax.rem(my_row + n_row - k, n_row)
        here = iota((steps, nb), 0) == source
        dest = jnp.sum(jnp.where(here, move_ref[:steps, :] + 1, 0), axis=0, keepdims=True) - 1
        rank = jnp.sum(jnp.where(here, move_ref[steps : 2 * steps, :], 0), axis=0, keepdims=True)
        place = jnp.sum(
            jnp.where(here, move_ref[2 * steps : 3 * steps, :], 0), axis=0, keepdims=True
        )
        key = jnp.where(dest == my_row, rank, -1)
        hot = one_hot(key == iota((MOVE_SLOTS, nb), 0))
        row = iota((8, nb), 0)
        parts = jnp.where(row == 0, place // 128, jnp.where(row == 1, place % 128, 1))
        found = lax.dot_general(
            parts.astype(F32).astype(BF16), hot, (((1,), (1,)), ((), ())),
            preferred_element_type=F32,
        )
        at = found[0:1] * 128.0 + found[1:2]
        targets.append(jnp.where(found[2:3] > 0.5, at, -1.0).astype(I32))
    target = jnp.concatenate(targets, axis=1)
    for k in range(local_rows // nb):
        rows = slice(k * nb, (k + 1) * nb)
        hit = iota((nb, n_row * MOVE_SLOTS), 0) + k * nb == target
        moved = dot(one_hot(hit), slots[...]).astype(BF16)
        any_hit = jnp.sum(jnp.where(hit, 1.0, 0.0), axis=1, keepdims=True) > 0.5
        value = jnp.where(any_hit, moved, res_ref[rows, :])
        if k == 0:
            value = jnp.where(my_row < steps, top_ref[...], value)
        out_ref[rows, :] = value


def call(kernel, outs, ins, scratch=(), any_at=()):
    vmem = pl.BlockSpec(memory_space=pltpu.VMEM)
    anywhere = pl.BlockSpec(memory_space=pl.ANY)
    return pl.pallas_call(
        kernel,
        out_shape=outs,
        in_specs=[anywhere if i in any_at else vmem for i in range(len(ins))],
        out_specs=jax.tree.map(lambda _: vmem, outs),
        scratch_shapes=list(scratch),
        compiler_params=pltpu.CompilerParams(vmem_limit_bytes=VMEM_BYTES),
    )(*ins)


def shape(*dims, dtype=BF16):
    return jax.ShapeDtypeStruct(dims, dtype)


def local(matrix, pivots, lower_inverse, upper_inverse):
    row_blocks, nb, col_blocks, _ = matrix.shape
    steps = pivots.shape[0]
    n_row = lax.axis_size("prow")
    n_col = lax.axis_size("pcol")
    if steps != 4 or col_blocks != 2 or n_row < steps or n_col < 8 or n_col % 4:
        return stepwise(matrix, pivots, lower_inverse, upper_inverse)
    my_col = lax.axis_index("pcol")
    local_rows = row_blocks * nb
    cap = -(-(steps * nb // n_row + 64) // 16) * 16
    mat = jnp.transpose(matrix, (2, 0, 1, 3)).reshape(col_blocks, local_rows, nb)
    m0 = mat[0]

    def from_panels(value, mask):
        return lax.ppermute(value, "pcol", [(i, i ^ mask) for i in range(steps)])

    def swap_cores(value):
        return lax.ppermute(value, "pcol", [(i, i ^ 1) for i in range(n_col)])

    on_panel = my_col < steps
    fours = range(4, n_col, 4)
    raw_x = from_panels(m0, 2)
    raw_far = functools.reduce(jnp.add, [from_panels(m0, mask) for mask in fours])

    meta, pack0, pack1 = call(
        functools.partial(pick_kernel, (nb, steps, n_row, cap, local_rows)),
        (shape(8, nb, dtype=I32), shape(cap, nb), shape(cap, nb)),
        (pivots, mat),
    )
    buf0 = lax.all_gather(pack0, "prow", tiled=True)
    buf0, raw_x, raw_far = lax.optimization_barrier((buf0, raw_x, raw_far))
    top0, off = call(
        functools.partial(order_kernel, (nb, steps)),
        (shape(steps * nb, nb), shape((steps - 1) * nb, nb)),
        (meta, buf0),
    )
    pack1, off = lax.optimization_barrier((pack1, off))
    off_x = from_panels(off, 2)
    off_far = functools.reduce(jnp.add, [from_panels(off, mask) for mask in fours])
    off_far_x = functools.reduce(jnp.add, [from_panels(off, mask + 2) for mask in fours])
    raw_far_x = lax.ppermute(raw_far, "pcol", [(i, i ^ 2) for i in range(steps, n_col)])
    buf1 = lax.all_gather(pack1, "prow", tiled=True)
    move = call(
        functools.partial(move_kernel, (nb, steps, n_row, cap)),
        shape(16, nb, dtype=I32),
        (pivots, meta),
    )
    buf1, off_far, raw_far_x = lax.optimization_barrier((buf1, off_far, raw_far_x))
    raw_0 = jnp.where(on_panel, m0, raw_far)
    raw_2 = jnp.where(on_panel, raw_x, raw_far_x)
    off_0 = jnp.where(on_panel, off, off_far)
    raw_1, raw_3, off_1 = swap_cores(raw_0), swap_cores(raw_2), swap_cores(off_0)
    buf1, off_x, off_far_x = lax.optimization_barrier((buf1, off_x, off_far_x))
    off_2 = jnp.where(on_panel, off_x, off_far_x)
    off_3 = swap_cores(off_2)
    top_rows = steps * nb
    res, top, send = call(
        functools.partial(factor_kernel, (nb, steps, n_row, local_rows)),
        (shape(local_rows, 2 * nb), shape(nb, 2 * nb), shape(n_row, MOVE_ROWS, 2 * nb)),
        (
            meta, move, top0, buf1, mat, raw_0, raw_2, raw_1, raw_3, off_0, off_2, off_1, off_3,
            lower_inverse, upper_inverse,
        ),
        scratch=(
            pltpu.VMEM((steps, local_rows, nb), BF16),
            pltpu.VMEM((steps, top_rows - nb, nb), BF16),
            pltpu.VMEM((local_rows, top_rows), BF16),
            pltpu.VMEM((top_rows, top_rows), BF16),
            pltpu.VMEM((top_rows, top_rows), BF16),
            pltpu.VMEM((top_rows, 2 * nb), BF16),
            pltpu.VMEM((top_rows, 2 * nb), BF16),
            pltpu.VMEM((top_rows, nb), BF16),
            pltpu.SemaphoreType.DMA((8,)),
        ),
        any_at=range(5, 13),
    )
    recv = [send[0]] + [
        lax.ppermute(send[k], "prow", [(i, (i + k) % n_row) for i in range(n_row)])
        for k in range(1, n_row)
    ]

    def finish():
        out = call(
            functools.partial(place_kernel, (nb, steps, n_row, local_rows)),
            shape(local_rows, 2 * nb),
            (move, res, top, *recv),
            scratch=(pltpu.VMEM((n_row * MOVE_SLOTS, 2 * nb), BF16),),
        )
        return out.reshape(matrix.shape)

    return lax.cond(
        move[3 * steps, 0] > 0,
        lambda: stepwise(matrix, pivots, lower_inverse, upper_inverse),
        finish,
    )


def solution(mesh):
    placed = (P(None, "prow", None, "pcol"), P(), P(), P())
    return jax.shard_map(
        local, mesh=mesh, in_specs=placed, out_specs=P(None, "prow", None, "pcol"), check_vma=False
    )
```

```python
import functools

import jax
import jax.numpy as jnp
from jax import lax
from jax.experimental import pallas as pl
from jax.experimental.pallas import tpu as pltpu
from jax.sharding import PartitionSpec as P

BF16 = jnp.bfloat16
F32 = jnp.float32
I32 = jnp.int32
VMEM_BYTES = 44 * 1024 * 1024
MOVE_ROWS = 80
MOVE_SLOTS = 128


def ring_sum(value, axis):
    size = lax.axis_size(axis)

    def turn(_, carry):
        total, passing = carry
        passing = lax.ppermute(passing, axis, [(i, (i + 1) % size) for i in range(size)])
        return total + passing, passing

    return lax.fori_loop(1, size, turn, (value, value))[0]


def spread(value, axis, source):
    kept = jnp.where(lax.axis_index(axis) == source, value, 0).astype(value.dtype)
    return ring_sum(kept, axis)


def stepwise(matrix, pivots, lower_inverse, upper_inverse):
    row_blocks = matrix.shape[0]
    block_size = matrix.shape[1]
    col_blocks = matrix.shape[2]
    local_rows = row_blocks * block_size
    local_cols = col_blocks * block_size
    matrix_loc = matrix.reshape(local_rows, local_cols)
    row_count = lax.axis_size("prow")
    col_count = lax.axis_size("pcol")
    my_row = lax.axis_index("prow")
    my_col = lax.axis_index("pcol")
    row_iota = jnp.arange(local_rows, dtype=jnp.int32)
    col_iota = jnp.arange(local_cols, dtype=jnp.int32)
    global_row = (row_iota // block_size * row_count + my_row) * block_size + row_iota % block_size
    global_col = (col_iota // block_size * col_count + my_col) * block_size + col_iota % block_size
    for step_num in range(pivots.shape[0]):
        begin_at = step_num * block_size
        trail_at = begin_at + block_size
        diag_root = step_num % row_count
        diag_local = step_num // row_count * block_size
        panel_root = step_num % col_count
        panel_local = step_num // col_count * block_size
        targets = begin_at + jnp.arange(block_size, dtype=jnp.int32)
        chosen = pivots[step_num]
        chosen_block = chosen // block_size
        chosen_owner = chosen_block % row_count
        is_mine = chosen_owner == my_row
        chosen_local = chosen_block // row_count * block_size + chosen % block_size
        picked = jnp.take(matrix_loc, jnp.where(is_mine, chosen_local, 0), axis=0)
        picked = jnp.where(is_mine[:, None], picked, jnp.zeros_like(picked))
        diag_rows = matrix_loc[diag_local : diag_local + block_size]
        own_diag = jnp.where(my_row == diag_root, diag_rows, jnp.zeros_like(diag_rows))
        new_rows, old_diag = ring_sum(picked, "prow"), ring_sum(own_diag, "prow")
        moved_rows = is_mine & (chosen != targets)
        matrix_loc = matrix_loc.at[jnp.where(moved_rows, chosen_local, local_rows)].set(
            old_diag, mode="drop"
        )
        diag_after = matrix_loc[diag_local : diag_local + block_size]
        matrix_loc = matrix_loc.at[diag_local : diag_local + block_size].set(
            jnp.where(my_row == diag_root, new_rows, diag_after)
        )
        upper_full = jnp.dot(
            lower_inverse[step_num], new_rows, preferred_element_type=jnp.float32
        ).astype(jnp.bfloat16)
        col_live = global_col >= trail_at
        upper_use = jnp.where(col_live[None, :], upper_full, jnp.zeros_like(upper_full))
        panel_own = matrix_loc[:, panel_local : panel_local + block_size]
        received = spread(panel_own, "pcol", panel_root)
        left_full = jnp.dot(
            received, upper_inverse[step_num], preferred_element_type=jnp.float32
        ).astype(jnp.bfloat16)
        row_live = global_row >= trail_at
        left_use = jnp.where(row_live[:, None], left_full, jnp.zeros_like(left_full))
        matrix_loc = (
            matrix_loc.astype(jnp.float32)
            - jnp.dot(left_use, upper_use, preferred_element_type=jnp.float32)
        ).astype(jnp.bfloat16)
        panel_now = matrix_loc[:, panel_local : panel_local + block_size]
        panel_put = jnp.where(row_live[:, None] & (my_col == panel_root), left_full, panel_now)
        matrix_loc = matrix_loc.at[:, panel_local : panel_local + block_size].set(panel_put)
        diag_now = matrix_loc[diag_local : diag_local + block_size]
        diag_put = jnp.where(col_live[None, :] & (my_row == diag_root), upper_full, diag_now)
        matrix_loc = matrix_loc.at[diag_local : diag_local + block_size].set(diag_put)
    return matrix_loc.reshape(matrix.shape)


def iota(shape, dim):
    return lax.broadcasted_iota(I32, shape, dim)


def dot(a, b):
    return jnp.dot(a, b, preferred_element_type=F32)


def one_hot(hit):
    return jnp.where(hit, 1.0, 0.0).astype(BF16)


def to_col(row, size):
    eye = iota((size, size), 0) == iota((size, size), 1)
    return jnp.sum(jnp.where(eye, jnp.broadcast_to(row, (size, size)), 0), axis=1, keepdims=True)


def find(col, base, x, size):
    hit = col == x
    place = jnp.sum(jnp.where(hit, iota((size, size), 0) + (base + 1), 0), axis=0, keepdims=True)
    return jnp.where(place > 0, place - 1, x)


def look(col, base, x, size):
    hit = iota((size, size), 0) + base == x
    return jnp.sum(jnp.where(hit, col, 0), axis=0, keepdims=True)


def before(rows, size):
    tri = one_hot(iota((size, size), 0) < iota((size, size), 1))
    stacked = jnp.concatenate([one_hot(r) for r in rows], axis=0)
    counts = dot(stacked, tri)
    k = rows[0].shape[0]
    return [counts[i * k : (i + 1) * k] for i in range(len(rows))]


def pick_kernel(cfg, piv_ref, mat_ref, meta_ref, pack0_ref, pack1_ref):
    nb, steps, n_row, cap, local_rows = cfg
    my_row = lax.axis_index("prow")
    piv = [piv_ref[t : t + 1, :] for t in range(steps)]
    cols = [to_col(piv[t], nb) for t in range(steps - 1)]
    owners, places = [], []
    for t in range(steps):
        x = piv[t]
        for s in range(t - 1, -1, -1):
            x = find(cols[s], s * nb, x, nb)
        block = x // nb
        owners.append(block % n_row)
        places.append(block // n_row * nb + x % nb)
    lanes = -(-n_row // 8) * 8
    member = [iota((lanes, nb), 0) == w for w in owners]
    counts = before(member, nb)
    base = jnp.zeros((lanes, 1), F32)
    ranks = []
    for t in range(steps):
        ranks.append(
            jnp.sum(jnp.where(member[t], counts[t] + base, 0.0), axis=0, keepdims=True).astype(I32)
        )
        base = base + jnp.sum(jnp.where(member[t], 1.0, 0.0), axis=1, keepdims=True)
    for t in range(steps):
        meta_ref[t : t + 1, :] = owners[t]
        meta_ref[steps + t : steps + t + 1, :] = ranks[t]
    over = jnp.max(base, axis=0, keepdims=True).astype(I32)
    meta_ref[2 * steps : 2 * steps + 1, :] = jnp.broadcast_to(over, (1, nb))
    slot = iota((cap, nb), 0)
    total = jnp.zeros((cap, nb), I32)
    for t in range(steps):
        key = jnp.where(owners[t] == my_row, ranks[t], -1)
        total = total + jnp.where(slot == key, places[t] + 1, 0)
    source = jnp.sum(total, axis=1, keepdims=True) - 1
    chosen = one_hot(source == iota((cap, local_rows), 1))
    pack0_ref[...] = dot(chosen, mat_ref[0]).astype(BF16)
    pack1_ref[...] = dot(chosen, mat_ref[1]).astype(BF16)


def find_moves(cfg, piv_ref, meta_ref, move_ref):
    nb, steps, n_row, cap = cfg
    piv = [piv_ref[t : t + 1, :] for t in range(steps)]
    cols = [to_col(piv[t], nb) for t in range(steps)]
    lanes = -(-n_row // 8) * 8
    dests, member = [], []
    for t in range(steps):
        at = iota((1, nb), 1) + t * nb
        x = at
        for s in range(t):
            x = find(cols[s], s * nb, x, nb)
        x = jnp.where(x == at, piv[t], x)
        for s in range(t + 1, steps):
            inside = (x >= s * nb) & (x < (s + 1) * nb)
            x = jnp.where(inside, look(cols[s], s * nb, x, nb), find(cols[s], s * nb, x, nb))
        block = x // nb
        dest = jnp.where(x >= steps * nb, block % n_row, -1)
        move_ref[t : t + 1, :] = dest
        move_ref[2 * steps + t : 2 * steps + t + 1, :] = block // n_row * nb + x % nb
        member.append(iota((lanes, nb), 0) == dest)
    counts = before(member, nb)
    most = jnp.zeros((lanes, 1), F32)
    for t in range(steps):
        move_ref[steps + t : steps + t + 1, :] = jnp.sum(
            jnp.where(member[t], counts[t], 0.0), axis=0, keepdims=True
        ).astype(I32)
        most = jnp.maximum(most, jnp.sum(jnp.where(member[t], 1.0, 0.0), axis=1, keepdims=True))
    over = jnp.max(most, axis=0, keepdims=True).astype(I32)
    bad = (over > MOVE_ROWS) | (meta_ref[2 * steps : 2 * steps + 1, :] > cap)
    move_ref[3 * steps : 3 * steps + 1, :] = jnp.where(bad, 1, 0)


def order_rows(pos, buf_ref):
    nb = pos.shape[1]
    hot = one_hot(to_col(pos, nb) == iota((nb, buf_ref.shape[0]), 1))
    return dot(hot, buf_ref[...]).astype(BF16)


def order_kernel(cfg, meta_ref, buf_ref, top_ref, off_ref):
    nb, steps, cap = cfg
    my_col = lax.axis_index("pcol")
    for t in range(steps):
        pos = meta_ref[t : t + 1, :] * cap + meta_ref[steps + t : steps + t + 1, :]
        top_ref[t * nb : (t + 1) * nb, :] = order_rows(pos, buf_ref)
    for j in range(steps - 1):
        block = jnp.where(my_col <= j, j + 1, j)
        rows = pl.ds(pl.multiple_of(block * nb, nb), nb)
        off_ref[j * nb : (j + 1) * nb, :] = top_ref[rows, :]


def late_kernel(cfg, piv_ref, meta_ref, buf_ref, move_ref, top_ref):
    nb, steps, n_row, cap = cfg
    find_moves(cfg, piv_ref, meta_ref, move_ref)
    for t in range(steps):
        pos = meta_ref[t : t + 1, :] * cap + meta_ref[steps + t : steps + t + 1, :]
        top_ref[t * nb : (t + 1) * nb, :] = order_rows(pos, buf_ref)


def fetch(panels, into, sems, first, rows):
    low = lax.axis_index("pcol") & 3
    copies = [
        pltpu.make_async_copy(panel.at[rows], into.at[low ^ mask], sems.at[first + mask])
        for mask, panel in enumerate(panels)
    ]
    for c in copies:
        c.start()
    return copies


def corner_kernel(
    cfg, move_ref, top0_ref, top1_ref, mat_ref, raws, offs, linv_ref, uinv_ref,
    upper, res_ref, top_ref, send_ref, raw, off, left, diag, sems,
):
    nb, steps, n_row = cfg
    wide = steps * nb
    my_row = lax.axis_index("prow")
    my_col = lax.axis_index("pcol")
    copies = fetch(offs, off, sems, 0, pl.ds(0, wide - nb))
    copies += fetch(raws, raw, sems, 4, pl.ds(0, nb))
    for c in copies:
        c.wait()
    for t in range(steps):
        here = slice(t * nb, (t + 1) * nb)
        done = slice(0, t * nb)
        parts = [off[j, here, :] for j in range(t + 1, steps)]
        parts += [top0_ref[here, :], top1_ref[here, :]]
        column = [off[t, t * nb :, :]] if t < steps - 1 else []
        column += [raw[t]]
        if t > 0:
            prod = dot(left[here, done], upper[done, (t + 1) * nb :])
            parts = [
                (p.astype(F32) - prod[:, i * nb : (i + 1) * nb]).astype(BF16)
                for i, p in enumerate(parts)
            ]
            prod = dot(left[(t + 1) * nb :, done], upper[done, here])
            at = 0
            for i, p in enumerate(column):
                rows = p.shape[0]
                column[i] = (p.astype(F32) - prod[at : at + rows]).astype(BF16)
                at += rows
        diag[here, :] = parts[-2]
        upper[here, (t + 1) * nb :] = dot(linv_ref[t], jnp.concatenate(parts, axis=1)).astype(BF16)
        left[(t + 1) * nb :, here] = dot(jnp.concatenate(column, axis=0), uinv_ref[t]).astype(BF16)
    in_panel = my_col < steps
    panel = pl.ds(pl.multiple_of(jnp.minimum(my_col, steps - 1) * nb, nb), nb)
    prod = dot(left[wide:, :], upper[:, wide:])
    value = (mat_ref[0, :nb, :].astype(F32) - prod[:, :nb]).astype(BF16)
    res_ref[:, :nb] = jnp.where(in_panel, left[wide:, panel], value)
    res_ref[:, nb:] = (mat_ref[1, :nb, :].astype(F32) - prod[:, nb:]).astype(BF16)
    here = iota((steps, nb), 0) == my_row
    dest = jnp.sum(jnp.where(here, move_ref[:steps, :] + 1, 0), axis=0, keepdims=True) - 1
    rank = jnp.sum(jnp.where(here, move_ref[steps : 2 * steps, :], 0), axis=0, keepdims=True)
    for k in range(n_row):
        key = jnp.where(dest == lax.rem(my_row + k, n_row), rank, -1)
        hot = one_hot(key == iota((MOVE_ROWS, nb), 0))
        send_ref[k] = dot(hot, res_ref[...]).astype(BF16)
    block = pl.ds(pl.multiple_of(jnp.minimum(my_row, steps - 1) * nb, nb), nb)
    value = jnp.where(my_col == my_row, diag[block, :], upper[block, wide : wide + nb])
    value = jnp.where(in_panel & (my_col < my_row), left[block, panel], value)
    top_ref[:, :nb] = value
    top_ref[:, nb:] = upper[block, wide + nb :]


def rows_kernel(
    cfg, mat_ref, raws, upper, uinv_ref, res_ref, raw, l_own, sems
):
    nb, steps, local_rows = cfg
    my_col = lax.axis_index("pcol")
    copies = fetch(raws, raw, sems, 0, pl.ds(nb, local_rows - nb))
    for c in copies:
        c.wait()
    tiles = [slice(k * nb, (k + 1) * nb) for k in range(local_rows // nb - 1)]
    for t in range(steps):
        here = slice(t * nb, (t + 1) * nb)
        done = slice(0, t * nb)
        for rows in tiles:
            acc = raw[t, rows, :].astype(F32)
            if t > 0:
                acc = acc - dot(l_own[rows, done], upper[done, here])
            l_own[rows, here] = dot(acc.astype(BF16), uinv_ref[t]).astype(BF16)
    in_panel = my_col < steps
    panel = pl.ds(pl.multiple_of(jnp.minimum(my_col, steps - 1) * nb, nb), nb)
    for rows in tiles:
        prod = dot(l_own[rows, :], upper[:, steps * nb :])
        source = slice(rows.start + nb, rows.stop + nb)
        left = (mat_ref[0, source, :].astype(F32) - prod[:, :nb]).astype(BF16)
        res_ref[rows, :nb] = jnp.where(in_panel, l_own[rows, panel], left)
        res_ref[rows, nb:] = (mat_ref[1, source, :].astype(F32) - prod[:, nb:]).astype(BF16)


def place_kernel(cfg, move_ref, head_ref, res_ref, top_ref, *refs):
    nb, steps, n_row, local_rows = cfg
    recv, out_ref, slots = refs[:n_row], refs[n_row], refs[n_row + 1]
    my_row = lax.axis_index("prow")
    slots[...] = jnp.zeros_like(slots)
    targets = []
    for k in range(n_row):
        slots[k * MOVE_SLOTS : k * MOVE_SLOTS + MOVE_ROWS, :] = recv[k][...]
        source = lax.rem(my_row + n_row - k, n_row)
        here = iota((steps, nb), 0) == source
        dest = jnp.sum(jnp.where(here, move_ref[:steps, :] + 1, 0), axis=0, keepdims=True) - 1
        rank = jnp.sum(jnp.where(here, move_ref[steps : 2 * steps, :], 0), axis=0, keepdims=True)
        place = jnp.sum(
            jnp.where(here, move_ref[2 * steps : 3 * steps, :], 0), axis=0, keepdims=True
        )
        key = jnp.where(dest == my_row, rank, -1)
        hot = one_hot(key == iota((MOVE_SLOTS, nb), 0))
        row = iota((8, nb), 0)
        parts = jnp.where(row == 0, place // 128, jnp.where(row == 1, place % 128, 1))
        found = lax.dot_general(
            parts.astype(F32).astype(BF16), hot, (((1,), (1,)), ((), ())),
            preferred_element_type=F32,
        )
        at = found[0:1] * 128.0 + found[1:2]
        targets.append(jnp.where(found[2:3] > 0.5, at, -1.0).astype(I32))
    target = jnp.concatenate(targets, axis=1)
    for k in range(local_rows // nb):
        rows = slice(k * nb, (k + 1) * nb)
        hit = iota((nb, n_row * MOVE_SLOTS), 0) + k * nb == target
        moved = dot(one_hot(hit), slots[...]).astype(BF16)
        any_hit = jnp.sum(jnp.where(hit, 1.0, 0.0), axis=1, keepdims=True) > 0.5
        if k == 0:
            value = jnp.where(any_hit, moved, head_ref[...])
            value = jnp.where(my_row < steps, top_ref[...], value)
        else:
            value = jnp.where(any_hit, moved, res_ref[(k - 1) * nb : k * nb, :])
        out_ref[rows, :] = value


def call(kernel, outs, ins, scratch=(), any_at=(), flops=None):
    vmem = pl.BlockSpec(memory_space=pltpu.VMEM)
    anywhere = pl.BlockSpec(memory_space=pl.ANY)
    return pl.pallas_call(
        kernel,
        out_shape=outs,
        in_specs=[
            jax.tree.map(lambda _: anywhere if i in any_at else vmem, x) for i, x in enumerate(ins)
        ],
        out_specs=jax.tree.map(lambda _: vmem, outs),
        scratch_shapes=list(scratch),
        compiler_params=pltpu.CompilerParams(vmem_limit_bytes=VMEM_BYTES),
        cost_estimate=flops
        and pl.CostEstimate(flops=flops, bytes_accessed=1 << 22, transcendentals=0),
    )(*ins)


def shape(*dims, dtype=BF16):
    return jax.ShapeDtypeStruct(dims, dtype)


def local(matrix, pivots, lower_inverse, upper_inverse):
    row_blocks, nb, col_blocks, _ = matrix.shape
    steps = pivots.shape[0]
    n_row = lax.axis_size("prow")
    n_col = lax.axis_size("pcol")
    if steps != 4 or col_blocks != 2 or n_row < steps or n_col < 8 or n_col % 4:
        return stepwise(matrix, pivots, lower_inverse, upper_inverse)
    local_rows = row_blocks * nb
    cap = -(-(steps * nb // n_row + 64) // 16) * 16
    mat = jnp.transpose(matrix, (2, 0, 1, 3)).reshape(col_blocks, local_rows, nb)
    m0 = mat[0]

    def from_panels(value, mask):
        return lax.ppermute(value, "pcol", [(i, i ^ mask) for i in range(steps)])

    def swap_cores(value):
        return lax.ppermute(value, "pcol", [(i, i ^ 1) for i in range(n_col)])

    def panel_pair(own, beside, far, far_beside):
        return jnp.where(on_panel, own, far), jnp.where(on_panel, beside, far_beside)

    on_panel = lax.axis_index("pcol") < steps
    fours = range(4, n_col, 4)
    raw_x = from_panels(m0, 2)
    raw_far = functools.reduce(jnp.add, [from_panels(m0, mask) for mask in fours])

    meta, pack0, pack1 = call(
        functools.partial(pick_kernel, (nb, steps, n_row, cap, local_rows)),
        (shape(16, nb, dtype=I32), shape(cap, nb), shape(cap, nb)),
        (pivots, mat),
    )
    buf0 = lax.all_gather(pack0, "prow", tiled=True)
    buf0, raw_x, raw_far = lax.optimization_barrier((buf0, raw_x, raw_far))
    top0, off = call(
        functools.partial(order_kernel, (nb, steps, cap)),
        (shape(steps * nb, nb), shape((steps - 1) * nb, nb)),
        (meta, buf0),
    )
    pack1, off, raw_far = lax.optimization_barrier((pack1, off, raw_far))
    off_x = from_panels(off, 2)
    off_far = functools.reduce(jnp.add, [from_panels(off, mask) for mask in fours])
    off_far_x = functools.reduce(jnp.add, [from_panels(off, mask + 2) for mask in fours])
    raw_far_x = lax.ppermute(raw_far, "pcol", [(i, i ^ 2) for i in range(steps, n_col)])
    buf1 = lax.all_gather(pack1, "prow", tiled=True)
    buf1, off_far, off_x, off_far_x = lax.optimization_barrier((buf1, off_far, off_x, off_far_x))
    raw_0, raw_2 = panel_pair(m0, raw_x, raw_far, raw_far_x)
    off_0, off_2 = panel_pair(off, off_x, off_far, off_far_x)
    raws = (raw_0, swap_cores(raw_0), raw_2, swap_cores(raw_2))
    offs = (off_0, swap_cores(off_0), off_2, swap_cores(off_2))
    move, top1 = call(
        functools.partial(late_kernel, (nb, steps, n_row, cap)),
        (shape(16, nb, dtype=I32), shape(steps * nb, nb)),
        (pivots, meta, buf1),
    )
    top_rows = steps * nb
    upper, head, top, send = call(
        functools.partial(corner_kernel, (nb, steps, n_row)),
        (
            shape(top_rows, top_rows + 2 * nb), shape(nb, 2 * nb), shape(nb, 2 * nb),
            shape(n_row, MOVE_ROWS, 2 * nb),
        ),
        (move, top0, top1, mat, raws, offs, lower_inverse, upper_inverse),
        scratch=(
            pltpu.VMEM((steps, nb, nb), BF16),
            pltpu.VMEM((steps, top_rows - nb, nb), BF16),
            pltpu.VMEM((top_rows + nb, top_rows), BF16),
            pltpu.VMEM((top_rows, nb), BF16),
            pltpu.SemaphoreType.DMA((8,)),
        ),
        any_at=(4, 5),
    )
    recv = [send[0]] + [
        lax.ppermute(send[k], "prow", [(i, (i + k) % n_row) for i in range(n_row)])
        for k in range(1, n_row)
    ]

    below = local_rows - nb
    res = call(
        functools.partial(rows_kernel, (nb, steps, local_rows)),
        shape(below, 2 * nb),
        (mat, raws, upper, upper_inverse),
        scratch=(
            pltpu.VMEM((steps, below, nb), BF16),
            pltpu.VMEM((below, top_rows), BF16),
            pltpu.SemaphoreType.DMA((4,)),
        ),
        any_at=(1,),
        flops=2 * below * top_rows * (top_rows + 2 * nb),
    )

    def finish():
        out = call(
            functools.partial(place_kernel, (nb, steps, n_row, local_rows)),
            shape(local_rows, 2 * nb),
            (move, head, res, top, *recv),
            scratch=(pltpu.VMEM((n_row * MOVE_SLOTS, 2 * nb), BF16),),
        )
        return out.reshape(matrix.shape)

    return lax.cond(
        move[3 * steps, 0] > 0,
        lambda: stepwise(matrix, pivots, lower_inverse, upper_inverse),
        finish,
    )


def solution(mesh):
    placed = (P(None, "prow", None, "pcol"), P(), P(), P())
    return jax.shard_map(
        local, mesh=mesh, in_specs=placed, out_specs=P(None, "prow", None, "pcol"), check_vma=False
    )
```

```python
import functools

import jax
import jax.numpy as jnp
from jax import lax
from jax.experimental import pallas as pl
from jax.experimental.pallas import tpu as pltpu
from jax.sharding import PartitionSpec as P

BF16 = jnp.bfloat16
F32 = jnp.float32
I32 = jnp.int32
VMEM_BYTES = 24 * 1024 * 1024
MOVE_ROWS = 80
MOVE_SLOTS = 128


def ring_sum(value, axis):
    size = lax.axis_size(axis)

    def turn(_, carry):
        total, passing = carry
        passing = lax.ppermute(passing, axis, [(i, (i + 1) % size) for i in range(size)])
        return total + passing, passing

    return lax.fori_loop(1, size, turn, (value, value))[0]


def spread(value, axis, source):
    kept = jnp.where(lax.axis_index(axis) == source, value, 0).astype(value.dtype)
    return ring_sum(kept, axis)


def stepwise(matrix, pivots, lower_inverse, upper_inverse):
    row_blocks = matrix.shape[0]
    block_size = matrix.shape[1]
    col_blocks = matrix.shape[2]
    local_rows = row_blocks * block_size
    local_cols = col_blocks * block_size
    matrix_loc = matrix.reshape(local_rows, local_cols)
    row_count = lax.axis_size("prow")
    col_count = lax.axis_size("pcol")
    my_row = lax.axis_index("prow")
    my_col = lax.axis_index("pcol")
    row_iota = jnp.arange(local_rows, dtype=jnp.int32)
    col_iota = jnp.arange(local_cols, dtype=jnp.int32)
    global_row = (row_iota // block_size * row_count + my_row) * block_size + row_iota % block_size
    global_col = (col_iota // block_size * col_count + my_col) * block_size + col_iota % block_size
    for step_num in range(pivots.shape[0]):
        begin_at = step_num * block_size
        trail_at = begin_at + block_size
        diag_root = step_num % row_count
        diag_local = step_num // row_count * block_size
        panel_root = step_num % col_count
        panel_local = step_num // col_count * block_size
        targets = begin_at + jnp.arange(block_size, dtype=jnp.int32)
        chosen = pivots[step_num]
        chosen_block = chosen // block_size
        chosen_owner = chosen_block % row_count
        is_mine = chosen_owner == my_row
        chosen_local = chosen_block // row_count * block_size + chosen % block_size
        picked = jnp.take(matrix_loc, jnp.where(is_mine, chosen_local, 0), axis=0)
        picked = jnp.where(is_mine[:, None], picked, jnp.zeros_like(picked))
        diag_rows = matrix_loc[diag_local : diag_local + block_size]
        own_diag = jnp.where(my_row == diag_root, diag_rows, jnp.zeros_like(diag_rows))
        new_rows, old_diag = ring_sum(picked, "prow"), ring_sum(own_diag, "prow")
        moved_rows = is_mine & (chosen != targets)
        matrix_loc = matrix_loc.at[jnp.where(moved_rows, chosen_local, local_rows)].set(
            old_diag, mode="drop"
        )
        diag_after = matrix_loc[diag_local : diag_local + block_size]
        matrix_loc = matrix_loc.at[diag_local : diag_local + block_size].set(
            jnp.where(my_row == diag_root, new_rows, diag_after)
        )
        upper_full = jnp.dot(
            lower_inverse[step_num], new_rows, preferred_element_type=jnp.float32
        ).astype(jnp.bfloat16)
        col_live = global_col >= trail_at
        upper_use = jnp.where(col_live[None, :], upper_full, jnp.zeros_like(upper_full))
        panel_own = matrix_loc[:, panel_local : panel_local + block_size]
        received = spread(panel_own, "pcol", panel_root)
        left_full = jnp.dot(
            received, upper_inverse[step_num], preferred_element_type=jnp.float32
        ).astype(jnp.bfloat16)
        row_live = global_row >= trail_at
        left_use = jnp.where(row_live[:, None], left_full, jnp.zeros_like(left_full))
        matrix_loc = (
            matrix_loc.astype(jnp.float32)
            - jnp.dot(left_use, upper_use, preferred_element_type=jnp.float32)
        ).astype(jnp.bfloat16)
        panel_now = matrix_loc[:, panel_local : panel_local + block_size]
        panel_put = jnp.where(row_live[:, None] & (my_col == panel_root), left_full, panel_now)
        matrix_loc = matrix_loc.at[:, panel_local : panel_local + block_size].set(panel_put)
        diag_now = matrix_loc[diag_local : diag_local + block_size]
        diag_put = jnp.where(col_live[None, :] & (my_row == diag_root), upper_full, diag_now)
        matrix_loc = matrix_loc.at[diag_local : diag_local + block_size].set(diag_put)
    return matrix_loc.reshape(matrix.shape)


def iota(shape, dim):
    return lax.broadcasted_iota(I32, shape, dim)


def dot(a, b):
    return jnp.dot(a, b, preferred_element_type=F32)


def one_hot(hit):
    return jnp.where(hit, 1.0, 0.0).astype(BF16)


def to_col(row, size):
    eye = iota((size, size), 0) == iota((size, size), 1)
    return jnp.sum(jnp.where(eye, jnp.broadcast_to(row, (size, size)), 0), axis=1, keepdims=True)


def find(col, base, x, size):
    hit = col == x
    place = jnp.sum(jnp.where(hit, iota((size, size), 0) + (base + 1), 0), axis=0, keepdims=True)
    return jnp.where(place > 0, place - 1, x)


def look(col, base, x, size):
    hit = iota((size, size), 0) + base == x
    return jnp.sum(jnp.where(hit, col, 0), axis=0, keepdims=True)


def before(rows, size):
    tri = one_hot(iota((size, size), 0) < iota((size, size), 1))
    stacked = jnp.concatenate([one_hot(r) for r in rows], axis=0)
    counts = dot(stacked, tri)
    k = rows[0].shape[0]
    return [counts[i * k : (i + 1) * k] for i in range(len(rows))]


def pick_kernel(cfg, piv_ref, mat_ref, meta_ref, pack0_ref, pack1_ref):
    nb, steps, n_row, cap, local_rows = cfg
    my_row = lax.axis_index("prow")
    piv = [piv_ref[t : t + 1, :] for t in range(steps)]
    cols = [to_col(piv[t], nb) for t in range(steps - 1)]
    owners, places = [], []
    for t in range(steps):
        x = piv[t]
        for s in range(t - 1, -1, -1):
            x = find(cols[s], s * nb, x, nb)
        block = x // nb
        owners.append(block % n_row)
        places.append(block // n_row * nb + x % nb)
    lanes = -(-n_row // 8) * 8
    member = [iota((lanes, nb), 0) == w for w in owners]
    counts = before(member, nb)
    base = jnp.zeros((lanes, 1), F32)
    ranks = []
    for t in range(steps):
        ranks.append(
            jnp.sum(jnp.where(member[t], counts[t] + base, 0.0), axis=0, keepdims=True).astype(I32)
        )
        base = base + jnp.sum(jnp.where(member[t], 1.0, 0.0), axis=1, keepdims=True)
    for t in range(steps):
        meta_ref[t : t + 1, :] = owners[t]
        meta_ref[steps + t : steps + t + 1, :] = ranks[t]
    over = jnp.max(base, axis=0, keepdims=True).astype(I32)
    meta_ref[2 * steps : 2 * steps + 1, :] = jnp.broadcast_to(over, (1, nb))
    slot = iota((cap, nb), 0)
    total = jnp.zeros((cap, nb), I32)
    for t in range(steps):
        key = jnp.where(owners[t] == my_row, ranks[t], -1)
        total = total + jnp.where(slot == key, places[t] + 1, 0)
    source = jnp.sum(total, axis=1, keepdims=True) - 1
    chosen = one_hot(source == iota((cap, local_rows), 1))
    pack0_ref[...] = dot(chosen, mat_ref[0]).astype(BF16)
    pack1_ref[...] = dot(chosen, mat_ref[1]).astype(BF16)


def final_places(x, piv_ref, cols, steps, size):
    for s in range(steps):
        base = s * size
        inside = (x >= base) & (x < base + size)
        x = jnp.where(inside, look(cols[s], base, x, size), find(cols[s], base, x, size))
    return x


def find_moves(cfg, piv_ref, meta_ref, move_ref):
    nb, steps, n_row, cap = cfg
    cols = [to_col(piv_ref[t : t + 1, :], nb) for t in range(steps)]
    lanes = -(-n_row // 8) * 8
    member = []
    for t in range(steps):
        x = final_places(iota((1, nb), 1) + t * nb, piv_ref, cols, steps, nb)
        block = x // nb
        dest = jnp.where(x >= steps * nb, block % n_row, -1)
        move_ref[t : t + 1, :] = dest
        move_ref[2 * steps + t : 2 * steps + t + 1, :] = block // n_row * nb + x % nb
        member.append(iota((lanes, nb), 0) == dest)
    counts = before(member, nb)
    most = jnp.zeros((lanes, 1), F32)
    for t in range(steps):
        move_ref[steps + t : steps + t + 1, :] = jnp.sum(
            jnp.where(member[t], counts[t], 0.0), axis=0, keepdims=True
        ).astype(I32)
        most = jnp.maximum(most, jnp.sum(jnp.where(member[t], 1.0, 0.0), axis=1, keepdims=True))
    over = jnp.max(most, axis=0, keepdims=True).astype(I32)
    bad = (over > MOVE_ROWS) | (meta_ref[2 * steps : 2 * steps + 1, :] > cap)
    return jnp.where(bad, 1, 0)


def find_targets(cfg, move_ref, my_row):
    nb, steps, n_row = cfg
    targets = []
    for k in range(n_row):
        here = iota((steps, nb), 0) == lax.rem(my_row + n_row - k, n_row)
        dest = jnp.sum(jnp.where(here, move_ref[:steps, :] + 1, 0), axis=0, keepdims=True) - 1
        rank = jnp.sum(jnp.where(here, move_ref[steps : 2 * steps, :], 0), axis=0, keepdims=True)
        place = jnp.sum(
            jnp.where(here, move_ref[2 * steps : 3 * steps, :], 0), axis=0, keepdims=True
        )
        key = jnp.where(dest == my_row, rank, -1)
        hot = one_hot(key == iota((MOVE_SLOTS, nb), 0))
        row = iota((8, nb), 0)
        parts = jnp.where(row == 0, place // 128, jnp.where(row == 1, place % 128, 1))
        found = lax.dot_general(
            parts.astype(F32).astype(BF16), hot, (((1,), (1,)), ((), ())),
            preferred_element_type=F32,
        )
        at = found[0:1] * 128.0 + found[1:2]
        targets.append(jnp.where(found[2:3] > 0.5, at, -1.0).astype(I32))
    return jnp.concatenate(targets, axis=1)


def order_rows(pos, buf_ref):
    nb = pos.shape[1]
    hot = one_hot(to_col(pos, nb) == iota((nb, buf_ref.shape[0]), 1))
    return dot(hot, buf_ref[...]).astype(BF16)


def order_kernel(cfg, meta_ref, buf_ref, top_ref, off_ref):
    nb, steps, cap = cfg
    my_col = lax.axis_index("pcol")
    for t in range(steps):
        pos = meta_ref[t : t + 1, :] * cap + meta_ref[steps + t : steps + t + 1, :]
        top_ref[t * nb : (t + 1) * nb, :] = order_rows(pos, buf_ref)
    for j in range(steps - 1):
        block = jnp.where(my_col <= j, j + 1, j)
        rows = pl.ds(pl.multiple_of(block * nb, nb), nb)
        off_ref[j * nb : (j + 1) * nb, :] = top_ref[rows, :]


def second_kernel(cfg, meta_ref, buf_ref, top_ref):
    nb, steps, cap = cfg
    for t in range(steps):
        pos = meta_ref[t : t + 1, :] * cap + meta_ref[steps + t : steps + t + 1, :]
        top_ref[t * nb : (t + 1) * nb, :] = order_rows(pos, buf_ref)


def sort_panels(panels, into, rows):
    low = lax.axis_index("pcol") & 3
    for mask, panel in enumerate(panels):
        into[low ^ mask] = panel[rows, :]


def corner_kernel(
    cfg, piv_ref, top0_ref, top1_ref, mat_ref, raws, offs, linv_hbm, uinv_ref,
    upper, res_ref, top_ref, send_ref, raw, off, left, diag, linv_ref, sem,
):
    nb, steps, n_row = cfg
    wide = steps * nb
    my_row = lax.axis_index("prow")
    my_col = lax.axis_index("pcol")
    load = pltpu.make_async_copy(linv_hbm, linv_ref, sem)
    load.start()
    sort_panels(offs, off, slice(0, wide - nb))
    sort_panels(raws, raw, slice(0, nb))
    load.wait()
    for t in range(steps):
        here = slice(t * nb, (t + 1) * nb)
        done = slice(0, t * nb)
        parts = [off[j, here, :] for j in range(t + 1, steps)]
        parts += [top0_ref[here, :], top1_ref[here, :]]
        column = [off[t, t * nb :, :]] if t < steps - 1 else []
        column += [raw[t]]
        if t > 0:
            prod = dot(left[here, done], upper[done, (t + 1) * nb :])
            parts = [
                (p.astype(F32) - prod[:, i * nb : (i + 1) * nb]).astype(BF16)
                for i, p in enumerate(parts)
            ]
            prod = dot(left[(t + 1) * nb :, done], upper[done, here])
            at = 0
            for i, p in enumerate(column):
                rows = p.shape[0]
                column[i] = (p.astype(F32) - prod[at : at + rows]).astype(BF16)
                at += rows
        diag[here, :] = parts[-2]
        upper[here, (t + 1) * nb :] = dot(linv_ref[t], jnp.concatenate(parts, axis=1)).astype(BF16)
        left[(t + 1) * nb :, here] = dot(jnp.concatenate(column, axis=0), uinv_ref[t]).astype(BF16)
    in_panel = my_col < steps
    panel = pl.ds(pl.multiple_of(jnp.minimum(my_col, steps - 1) * nb, nb), nb)
    prod = dot(left[wide:, :], upper[:, wide:])
    value = (mat_ref[0, :nb, :].astype(F32) - prod[:, :nb]).astype(BF16)
    res_ref[:, :nb] = jnp.where(in_panel, left[wide:, panel], value)
    res_ref[:, nb:] = (mat_ref[1, :nb, :].astype(F32) - prod[:, nb:]).astype(BF16)
    cols = [to_col(piv_ref[t : t + 1, :], nb) for t in range(steps)]
    x = final_places(iota((1, nb), 1) + my_row * nb, piv_ref, cols, steps, nb)
    dest = jnp.where((x >= wide) & (my_row < steps), x // nb % n_row, -1)
    member = iota((-(-n_row // 8) * 8, nb), 0) == dest
    rank = jnp.sum(jnp.where(member, before([member], nb)[0], 0.0), axis=0, keepdims=True)
    rank = rank.astype(I32)
    for k in range(n_row):
        key = jnp.where(dest == lax.rem(my_row + k, n_row), rank, -1)
        hot = one_hot(key == iota((MOVE_ROWS, nb), 0))
        send_ref[k] = dot(hot, res_ref[...]).astype(BF16)
    block = pl.ds(pl.multiple_of(jnp.minimum(my_row, steps - 1) * nb, nb), nb)
    value = jnp.where(my_col == my_row, diag[block, :], upper[block, wide : wide + nb])
    value = jnp.where(in_panel & (my_col < my_row), left[block, panel], value)
    top_ref[:, :nb] = value
    top_ref[:, nb:] = upper[block, wide + nb :]


def rows_kernel(
    cfg, piv_ref, meta_ref, mat_ref, raws, upper, uinv_ref, res_ref, target_ref,
    flag_ref, raw, l_own, move_ref,
):
    nb, steps, n_row, cap, local_rows = cfg
    my_col = lax.axis_index("pcol")
    sort_panels(raws, raw, slice(nb, local_rows))
    bad = find_moves((nb, steps, n_row, cap), piv_ref, meta_ref, move_ref)
    target_ref[...] = find_targets((nb, steps, n_row), move_ref, lax.axis_index("prow"))
    flag_ref[0] = jnp.max(bad)
    tiles = [slice(k * nb, (k + 1) * nb) for k in range(local_rows // nb - 1)]
    for t in range(steps):
        here = slice(t * nb, (t + 1) * nb)
        done = slice(0, t * nb)
        for rows in tiles:
            acc = raw[t, rows, :].astype(F32)
            if t > 0:
                acc = acc - dot(l_own[rows, done], upper[done, here])
            l_own[rows, here] = dot(acc.astype(BF16), uinv_ref[t]).astype(BF16)
    in_panel = my_col < steps
    panel = pl.ds(pl.multiple_of(jnp.minimum(my_col, steps - 1) * nb, nb), nb)
    for rows in tiles:
        prod = dot(l_own[rows, :], upper[:, steps * nb :])
        source = slice(rows.start + nb, rows.stop + nb)
        left = (mat_ref[0, source, :].astype(F32) - prod[:, :nb]).astype(BF16)
        res_ref[rows, :nb] = jnp.where(in_panel, l_own[rows, panel], left)
        res_ref[rows, nb:] = (mat_ref[1, source, :].astype(F32) - prod[:, nb:]).astype(BF16)


def place_kernel(cfg, target_ref, head_ref, res_ref, top_ref, *refs):
    nb, steps, n_row, local_rows = cfg
    recv, out_ref, slots = refs[:n_row], refs[n_row], refs[n_row + 1]
    my_row = lax.axis_index("prow")
    slots[...] = jnp.zeros_like(slots)
    for k in range(n_row):
        slots[k * MOVE_SLOTS : k * MOVE_SLOTS + MOVE_ROWS, :] = recv[k][...]
    target = target_ref[...]
    for k in range(local_rows // nb):
        rows = slice(k * nb, (k + 1) * nb)
        hit = iota((nb, n_row * MOVE_SLOTS), 0) + k * nb == target
        moved = dot(one_hot(hit), slots[...]).astype(BF16)
        any_hit = jnp.sum(jnp.where(hit, 1.0, 0.0), axis=1, keepdims=True) > 0.5
        if k == 0:
            value = jnp.where(any_hit, moved, head_ref[...])
            value = jnp.where(my_row < steps, top_ref[...], value)
        else:
            value = jnp.where(any_hit, moved, res_ref[(k - 1) * nb : k * nb, :])
        out_ref[rows, :] = value


def call(kernel, outs, ins, scratch=(), any_at=(), flops=None):
    vmem = pl.BlockSpec(memory_space=pltpu.VMEM)
    anywhere = pl.BlockSpec(memory_space=pl.ANY)
    scalars = pl.BlockSpec(memory_space=pltpu.SMEM)
    return pl.pallas_call(
        kernel,
        out_shape=outs,
        in_specs=[
            jax.tree.map(lambda _: anywhere if i in any_at else vmem, x) for i, x in enumerate(ins)
        ],
        out_specs=jax.tree.map(lambda x: scalars if x.shape == (1,) else vmem, outs),
        scratch_shapes=list(scratch),
        compiler_params=pltpu.CompilerParams(vmem_limit_bytes=VMEM_BYTES),
        cost_estimate=flops
        and pl.CostEstimate(flops=flops, bytes_accessed=1 << 22, transcendentals=0),
    )(*ins)


def shape(*dims, dtype=BF16):
    return jax.ShapeDtypeStruct(dims, dtype)


def local(matrix, pivots, lower_inverse, upper_inverse):
    row_blocks, nb, col_blocks, _ = matrix.shape
    steps = pivots.shape[0]
    n_row = lax.axis_size("prow")
    n_col = lax.axis_size("pcol")
    if steps != 4 or col_blocks != 2 or n_row < steps or n_col < 8 or n_col % 4:
        return stepwise(matrix, pivots, lower_inverse, upper_inverse)
    local_rows = row_blocks * nb
    cap = -(-(steps * nb // n_row + 64) // 16) * 16
    mat = jnp.transpose(matrix, (2, 0, 1, 3)).reshape(col_blocks, local_rows, nb)
    m0 = mat[0]

    def from_panels(value, mask):
        return lax.ppermute(value, "pcol", [(i, i ^ mask) for i in range(steps)])

    def swap_cores(value):
        return lax.ppermute(value, "pcol", [(i, i ^ 1) for i in range(n_col)])

    def panel_pair(own, beside, far, far_beside):
        return jnp.where(on_panel, own, far), jnp.where(on_panel, beside, far_beside)

    on_panel = lax.axis_index("pcol") < steps
    fours = range(4, n_col, 4)
    raw_x = from_panels(m0, 2)
    raw_far = functools.reduce(jnp.add, [from_panels(m0, mask) for mask in fours])

    meta, pack0, pack1 = call(
        functools.partial(pick_kernel, (nb, steps, n_row, cap, local_rows)),
        (shape(16, nb, dtype=I32), shape(cap, nb), shape(cap, nb)),
        (pivots, mat),
    )
    buf0 = lax.all_gather(pack0, "prow", tiled=True)
    buf0, raw_x, raw_far = lax.optimization_barrier((buf0, raw_x, raw_far))
    top0, off = call(
        functools.partial(order_kernel, (nb, steps, cap)),
        (shape(steps * nb, nb), shape((steps - 1) * nb, nb)),
        (meta, buf0),
    )
    pack1, off, raw_far = lax.optimization_barrier((pack1, off, raw_far))
    off_x = from_panels(off, 2)
    off_far = functools.reduce(jnp.add, [from_panels(off, mask) for mask in fours])
    off_far_x = functools.reduce(jnp.add, [from_panels(off, mask + 2) for mask in fours])
    raw_far_x = lax.ppermute(raw_far, "pcol", [(i, i ^ 2) for i in range(steps, n_col)])
    buf1 = lax.all_gather(pack1, "prow", tiled=True)
    buf1, off_far, off_x, off_far_x = lax.optimization_barrier((buf1, off_far, off_x, off_far_x))
    raw_0, raw_2 = panel_pair(m0, raw_x, raw_far, raw_far_x)
    off_0, off_2 = panel_pair(off, off_x, off_far, off_far_x)
    raws = (raw_0, swap_cores(raw_0), raw_2, swap_cores(raw_2))
    offs = (off_0, swap_cores(off_0), off_2, swap_cores(off_2))
    top1 = call(
        functools.partial(second_kernel, (nb, steps, cap)), shape(steps * nb, nb), (meta, buf1)
    )
    top_rows = steps * nb
    upper, head, top, send = call(
        functools.partial(corner_kernel, (nb, steps, n_row)),
        (
            shape(top_rows, top_rows + 2 * nb), shape(nb, 2 * nb), shape(nb, 2 * nb),
            shape(n_row, MOVE_ROWS, 2 * nb),
        ),
        (pivots, top0, top1, mat, raws, offs, lower_inverse, upper_inverse),
        scratch=(
            pltpu.VMEM((steps, nb, nb), BF16),
            pltpu.VMEM((steps, top_rows - nb, nb), BF16),
            pltpu.VMEM((top_rows + nb, top_rows), BF16),
            pltpu.VMEM((top_rows, nb), BF16),
            pltpu.VMEM((steps, nb, nb), BF16),
            pltpu.SemaphoreType.DMA,
        ),
        any_at=(6,),
    )
    recv = [send[0]] + [
        lax.ppermute(send[k], "prow", [(i, (i + k) % n_row) for i in range(n_row)])
        for k in range(1, n_row)
    ]

    below = local_rows - nb
    res, target, crowded = call(
        functools.partial(rows_kernel, (nb, steps, n_row, cap, local_rows)),
        (
            shape(below, 2 * nb), shape(1, n_row * MOVE_SLOTS, dtype=I32), shape(1, dtype=I32),
        ),
        (pivots, meta, mat, raws, upper, upper_inverse),
        scratch=(
            pltpu.VMEM((steps, below, nb), BF16),
            pltpu.VMEM((below, top_rows), BF16),
            pltpu.VMEM((16, nb), I32),
        ),
        flops=2 * below * top_rows * (top_rows + 2 * nb),
    )

    def finish():
        out = call(
            functools.partial(place_kernel, (nb, steps, n_row, local_rows)),
            shape(local_rows, 2 * nb),
            (target, head, res, top, *recv),
            scratch=(pltpu.VMEM((n_row * MOVE_SLOTS, 2 * nb), BF16),),
        )
        return out.reshape(matrix.shape)

    return lax.cond(
        crowded[0] > 0,
        lambda: stepwise(matrix, pivots, lower_inverse, upper_inverse),
        finish,
    )


def solution(mesh):
    placed = (P(None, "prow", None, "pcol"), P(), P(), P())
    return jax.shard_map(
        local, mesh=mesh, in_specs=placed, out_specs=P(None, "prow", None, "pcol"), check_vma=False
    )
```

```python
import functools

import jax
import jax.numpy as jnp
from jax import lax
from jax.experimental import pallas as pl
from jax.experimental.pallas import tpu as pltpu
from jax.sharding import PartitionSpec as P

BF16 = jnp.bfloat16
F32 = jnp.float32
I32 = jnp.int32
VMEM_BYTES = 24 * 1024 * 1024
MOVE_ROWS = 80
MOVE_SLOTS = 128


def ring_sum(value, axis):
    size = lax.axis_size(axis)

    def turn(_, carry):
        total, passing = carry
        passing = lax.ppermute(passing, axis, [(i, (i + 1) % size) for i in range(size)])
        return total + passing, passing

    return lax.fori_loop(1, size, turn, (value, value))[0]


def spread(value, axis, source):
    kept = jnp.where(lax.axis_index(axis) == source, value, 0).astype(value.dtype)
    return ring_sum(kept, axis)


def stepwise(matrix, pivots, lower_inverse, upper_inverse):
    row_blocks = matrix.shape[0]
    block_size = matrix.shape[1]
    col_blocks = matrix.shape[2]
    local_rows = row_blocks * block_size
    local_cols = col_blocks * block_size
    matrix_loc = matrix.reshape(local_rows, local_cols)
    row_count = lax.axis_size("prow")
    col_count = lax.axis_size("pcol")
    my_row = lax.axis_index("prow")
    my_col = lax.axis_index("pcol")
    row_iota = jnp.arange(local_rows, dtype=jnp.int32)
    col_iota = jnp.arange(local_cols, dtype=jnp.int32)
    global_row = (row_iota // block_size * row_count + my_row) * block_size + row_iota % block_size
    global_col = (col_iota // block_size * col_count + my_col) * block_size + col_iota % block_size
    for step_num in range(pivots.shape[0]):
        begin_at = step_num * block_size
        trail_at = begin_at + block_size
        diag_root = step_num % row_count
        diag_local = step_num // row_count * block_size
        panel_root = step_num % col_count
        panel_local = step_num // col_count * block_size
        targets = begin_at + jnp.arange(block_size, dtype=jnp.int32)
        chosen = pivots[step_num]
        chosen_block = chosen // block_size
        chosen_owner = chosen_block % row_count
        is_mine = chosen_owner == my_row
        chosen_local = chosen_block // row_count * block_size + chosen % block_size
        picked = jnp.take(matrix_loc, jnp.where(is_mine, chosen_local, 0), axis=0)
        picked = jnp.where(is_mine[:, None], picked, jnp.zeros_like(picked))
        diag_rows = matrix_loc[diag_local : diag_local + block_size]
        own_diag = jnp.where(my_row == diag_root, diag_rows, jnp.zeros_like(diag_rows))
        new_rows, old_diag = ring_sum(picked, "prow"), ring_sum(own_diag, "prow")
        moved_rows = is_mine & (chosen != targets)
        matrix_loc = matrix_loc.at[jnp.where(moved_rows, chosen_local, local_rows)].set(
            old_diag, mode="drop"
        )
        diag_after = matrix_loc[diag_local : diag_local + block_size]
        matrix_loc = matrix_loc.at[diag_local : diag_local + block_size].set(
            jnp.where(my_row == diag_root, new_rows, diag_after)
        )
        upper_full = jnp.dot(
            lower_inverse[step_num], new_rows, preferred_element_type=jnp.float32
        ).astype(jnp.bfloat16)
        col_live = global_col >= trail_at
        upper_use = jnp.where(col_live[None, :], upper_full, jnp.zeros_like(upper_full))
        panel_own = matrix_loc[:, panel_local : panel_local + block_size]
        received = spread(panel_own, "pcol", panel_root)
        left_full = jnp.dot(
            received, upper_inverse[step_num], preferred_element_type=jnp.float32
        ).astype(jnp.bfloat16)
        row_live = global_row >= trail_at
        left_use = jnp.where(row_live[:, None], left_full, jnp.zeros_like(left_full))
        matrix_loc = (
            matrix_loc.astype(jnp.float32)
            - jnp.dot(left_use, upper_use, preferred_element_type=jnp.float32)
        ).astype(jnp.bfloat16)
        panel_now = matrix_loc[:, panel_local : panel_local + block_size]
        panel_put = jnp.where(row_live[:, None] & (my_col == panel_root), left_full, panel_now)
        matrix_loc = matrix_loc.at[:, panel_local : panel_local + block_size].set(panel_put)
        diag_now = matrix_loc[diag_local : diag_local + block_size]
        diag_put = jnp.where(col_live[None, :] & (my_row == diag_root), upper_full, diag_now)
        matrix_loc = matrix_loc.at[diag_local : diag_local + block_size].set(diag_put)
    return matrix_loc.reshape(matrix.shape)


def iota(shape, dim):
    return lax.broadcasted_iota(I32, shape, dim)


def dot(a, b):
    return jnp.dot(a, b, preferred_element_type=F32)


def one_hot(hit):
    return jnp.where(hit, 1.0, 0.0).astype(BF16)


def to_col(row, size):
    eye = iota((size, size), 0) == iota((size, size), 1)
    return jnp.sum(jnp.where(eye, jnp.broadcast_to(row, (size, size)), 0), axis=1, keepdims=True)


def find(col, base, x, size):
    hit = col == x
    place = jnp.sum(jnp.where(hit, iota((size, size), 0) + (base + 1), 0), axis=0, keepdims=True)
    return jnp.where(place > 0, place - 1, x)


def look(col, base, x, size):
    hit = iota((size, size), 0) + base == x
    return jnp.sum(jnp.where(hit, col, 0), axis=0, keepdims=True)


def before(rows, size):
    tri = one_hot(iota((size, size), 0) < iota((size, size), 1))
    stacked = jnp.concatenate([one_hot(r) for r in rows], axis=0)
    counts = dot(stacked, tri)
    k = rows[0].shape[0]
    return [counts[i * k : (i + 1) * k] for i in range(len(rows))]


def pick_kernel(cfg, piv_ref, mat_ref, meta_ref, pack0_ref, pack1_ref):
    nb, steps, n_row, cap, local_rows = cfg
    my_row = lax.axis_index("prow")
    piv = [piv_ref[t : t + 1, :] for t in range(steps)]
    cols = [to_col(piv[t], nb) for t in range(steps - 1)]
    owners, places = [], []
    for t in range(steps):
        x = piv[t]
        for s in range(t - 1, -1, -1):
            x = find(cols[s], s * nb, x, nb)
        block = x // nb
        owners.append(block % n_row)
        places.append(block // n_row * nb + x % nb)
    lanes = -(-n_row // 8) * 8
    member = [iota((lanes, nb), 0) == w for w in owners]
    counts = before(member, nb)
    base = jnp.zeros((lanes, 1), F32)
    ranks = []
    for t in range(steps):
        ranks.append(
            jnp.sum(jnp.where(member[t], counts[t] + base, 0.0), axis=0, keepdims=True).astype(I32)
        )
        base = base + jnp.sum(jnp.where(member[t], 1.0, 0.0), axis=1, keepdims=True)
    for t in range(steps):
        meta_ref[t : t + 1, :] = owners[t]
        meta_ref[steps + t : steps + t + 1, :] = ranks[t]
    over = jnp.max(base, axis=0, keepdims=True).astype(I32)
    meta_ref[2 * steps : 2 * steps + 1, :] = jnp.broadcast_to(over, (1, nb))
    slot = iota((cap, nb), 0)
    total = jnp.zeros((cap, nb), I32)
    for t in range(steps):
        key = jnp.where(owners[t] == my_row, ranks[t], -1)
        total = total + jnp.where(slot == key, places[t] + 1, 0)
    source = jnp.sum(total, axis=1, keepdims=True) - 1
    chosen = one_hot(source == iota((cap, local_rows), 1))
    pack0_ref[...] = dot(chosen, mat_ref[0]).astype(BF16)
    pack1_ref[...] = dot(chosen, mat_ref[1]).astype(BF16)


def final_places(x, piv_ref, cols, steps, size):
    for s in range(steps):
        base = s * size
        inside = (x >= base) & (x < base + size)
        x = jnp.where(inside, look(cols[s], base, x, size), find(cols[s], base, x, size))
    return x


def find_moves(cfg, piv_ref, meta_ref, move_ref):
    nb, steps, n_row, cap = cfg
    cols = [to_col(piv_ref[t : t + 1, :], nb) for t in range(steps)]
    lanes = -(-n_row // 8) * 8
    member = []
    for t in range(steps):
        x = final_places(iota((1, nb), 1) + t * nb, piv_ref, cols, steps, nb)
        block = x // nb
        dest = jnp.where(x >= steps * nb, block % n_row, -1)
        move_ref[t : t + 1, :] = dest
        move_ref[2 * steps + t : 2 * steps + t + 1, :] = block // n_row * nb + x % nb
        member.append(iota((lanes, nb), 0) == dest)
    counts = before(member, nb)
    most = jnp.zeros((lanes, 1), F32)
    for t in range(steps):
        move_ref[steps + t : steps + t + 1, :] = jnp.sum(
            jnp.where(member[t], counts[t], 0.0), axis=0, keepdims=True
        ).astype(I32)
        most = jnp.maximum(most, jnp.sum(jnp.where(member[t], 1.0, 0.0), axis=1, keepdims=True))
    over = jnp.max(most, axis=0, keepdims=True).astype(I32)
    bad = (over > MOVE_ROWS) | (meta_ref[2 * steps : 2 * steps + 1, :] > cap)
    return jnp.where(bad, 1, 0)


def find_targets(cfg, move_ref, my_row):
    nb, steps, n_row = cfg
    targets = []
    for k in range(n_row):
        here = iota((steps, nb), 0) == lax.rem(my_row + n_row - k, n_row)
        dest = jnp.sum(jnp.where(here, move_ref[:steps, :] + 1, 0), axis=0, keepdims=True) - 1
        rank = jnp.sum(jnp.where(here, move_ref[steps : 2 * steps, :], 0), axis=0, keepdims=True)
        place = jnp.sum(
            jnp.where(here, move_ref[2 * steps : 3 * steps, :], 0), axis=0, keepdims=True
        )
        key = jnp.where(dest == my_row, rank, -1)
        hot = one_hot(key == iota((MOVE_SLOTS, nb), 0))
        row = iota((8, nb), 0)
        parts = jnp.where(row == 0, place // 128, jnp.where(row == 1, place % 128, 1))
        found = lax.dot_general(
            parts.astype(F32).astype(BF16), hot, (((1,), (1,)), ((), ())),
            preferred_element_type=F32,
        )
        at = found[0:1] * 128.0 + found[1:2]
        targets.append(jnp.where(found[2:3] > 0.5, at, -1.0).astype(I32))
    return jnp.concatenate(targets, axis=1)


def order_rows(pos, buf_ref):
    nb = pos.shape[1]
    hot = one_hot(to_col(pos, nb) == iota((nb, buf_ref.shape[0]), 1))
    return dot(hot, buf_ref[...]).astype(BF16)


def order_kernel(cfg, meta_ref, parts, top_ref, off_ref, buf):
    nb, steps, n_row, cap = cfg
    my_row = lax.axis_index("prow")
    my_col = lax.axis_index("pcol")
    for k in range(n_row):
        buf[k * cap : (k + 1) * cap, :] = parts[k][...]
    for t in range(steps):
        turn = my_row - meta_ref[t : t + 1, :]
        turn = jnp.where(turn < 0, turn + n_row, turn)
        pos = turn * cap + meta_ref[steps + t : steps + t + 1, :]
        top_ref[t * nb : (t + 1) * nb, :] = order_rows(pos, buf)
    for j in range(steps - 1):
        block = jnp.where(my_col <= j, j + 1, j)
        rows = pl.ds(pl.multiple_of(block * nb, nb), nb)
        off_ref[j * nb : (j + 1) * nb, :] = top_ref[rows, :]


def second_kernel(cfg, meta_ref, buf_ref, top_ref):
    nb, steps, cap = cfg
    for t in range(steps):
        pos = meta_ref[t : t + 1, :] * cap + meta_ref[steps + t : steps + t + 1, :]
        top_ref[t * nb : (t + 1) * nb, :] = order_rows(pos, buf_ref)


def sort_panels(panels, into, rows):
    low = lax.axis_index("pcol") & 3
    for mask, panel in enumerate(panels):
        into[low ^ mask] = panel[rows, :]


def corner_kernel(
    cfg, piv_ref, top0_ref, top1_ref, mat_ref, raws, offs, linv_hbm, uinv_ref,
    upper, res_ref, top_ref, send_ref, raw, off, left, diag, linv_ref, sem,
):
    nb, steps, n_row = cfg
    wide = steps * nb
    my_row = lax.axis_index("prow")
    my_col = lax.axis_index("pcol")
    load = pltpu.make_async_copy(linv_hbm, linv_ref, sem)
    load.start()
    sort_panels(offs, off, slice(0, wide - nb))
    sort_panels(raws, raw, slice(0, nb))
    load.wait()
    for t in range(steps):
        here = slice(t * nb, (t + 1) * nb)
        done = slice(0, t * nb)
        parts = [off[j, here, :] for j in range(t + 1, steps)]
        parts += [top0_ref[here, :], top1_ref[here, :]]
        column = [off[t, t * nb :, :]] if t < steps - 1 else []
        column += [raw[t]]
        if t > 0:
            prod = dot(left[here, done], upper[done, (t + 1) * nb :])
            parts = [
                (p.astype(F32) - prod[:, i * nb : (i + 1) * nb]).astype(BF16)
                for i, p in enumerate(parts)
            ]
            prod = dot(left[(t + 1) * nb :, done], upper[done, here])
            at = 0
            for i, p in enumerate(column):
                rows = p.shape[0]
                column[i] = (p.astype(F32) - prod[at : at + rows]).astype(BF16)
                at += rows
        diag[here, :] = parts[-2]
        upper[here, (t + 1) * nb :] = dot(linv_ref[t], jnp.concatenate(parts, axis=1)).astype(BF16)
        left[(t + 1) * nb :, here] = dot(jnp.concatenate(column, axis=0), uinv_ref[t]).astype(BF16)
    in_panel = my_col < steps
    panel = pl.ds(pl.multiple_of(jnp.minimum(my_col, steps - 1) * nb, nb), nb)
    prod = dot(left[wide:, :], upper[:, wide:])
    value = (mat_ref[0, :nb, :].astype(F32) - prod[:, :nb]).astype(BF16)
    res_ref[:, :nb] = jnp.where(in_panel, left[wide:, panel], value)
    res_ref[:, nb:] = (mat_ref[1, :nb, :].astype(F32) - prod[:, nb:]).astype(BF16)
    cols = [to_col(piv_ref[t : t + 1, :], nb) for t in range(steps)]
    x = final_places(iota((1, nb), 1) + my_row * nb, piv_ref, cols, steps, nb)
    dest = jnp.where((x >= wide) & (my_row < steps), x // nb % n_row, -1)
    member = iota((-(-n_row // 8) * 8, nb), 0) == dest
    rank = jnp.sum(jnp.where(member, before([member], nb)[0], 0.0), axis=0, keepdims=True)
    rank = rank.astype(I32)
    hot = []
    for k in range(n_row):
        key = jnp.where(dest == lax.rem(my_row + k, n_row), rank, -1)
        hot.append(one_hot(key == iota((MOVE_ROWS, nb), 0)))
    moved = dot(jnp.concatenate(hot, axis=0), res_ref[...]).astype(BF16)
    for k in range(n_row):
        send_ref[k] = moved[k * MOVE_ROWS : (k + 1) * MOVE_ROWS]
    block = pl.ds(pl.multiple_of(jnp.minimum(my_row, steps - 1) * nb, nb), nb)
    value = jnp.where(my_col == my_row, diag[block, :], upper[block, wide : wide + nb])
    value = jnp.where(in_panel & (my_col < my_row), left[block, panel], value)
    top_ref[:, :nb] = value
    top_ref[:, nb:] = upper[block, wide + nb :]


def rows_kernel(
    cfg, piv_ref, meta_ref, mat_ref, raws, upper, uinv_ref, res_ref, target_ref,
    flag_ref, raw, l_own, move_ref,
):
    nb, steps, n_row, cap, local_rows = cfg
    my_col = lax.axis_index("pcol")
    sort_panels(raws, raw, slice(nb, local_rows))
    bad = find_moves((nb, steps, n_row, cap), piv_ref, meta_ref, move_ref)
    target_ref[...] = find_targets((nb, steps, n_row), move_ref, lax.axis_index("prow"))
    flag_ref[0] = jnp.max(bad)
    tiles = [slice(k * nb, (k + 1) * nb) for k in range(local_rows // nb - 1)]
    for t in range(steps):
        here = slice(t * nb, (t + 1) * nb)
        done = slice(0, t * nb)
        for rows in tiles:
            acc = raw[t, rows, :].astype(F32)
            if t > 0:
                acc = acc - dot(l_own[rows, done], upper[done, here])
            l_own[rows, here] = dot(acc.astype(BF16), uinv_ref[t]).astype(BF16)
    in_panel = my_col < steps
    panel = pl.ds(pl.multiple_of(jnp.minimum(my_col, steps - 1) * nb, nb), nb)
    for rows in tiles:
        prod = dot(l_own[rows, :], upper[:, steps * nb :])
        source = slice(rows.start + nb, rows.stop + nb)
        left = (mat_ref[0, source, :].astype(F32) - prod[:, :nb]).astype(BF16)
        res_ref[rows, :nb] = jnp.where(in_panel, l_own[rows, panel], left)
        res_ref[rows, nb:] = (mat_ref[1, source, :].astype(F32) - prod[:, nb:]).astype(BF16)


def place_kernel(cfg, target_ref, head_ref, res_ref, top_ref, *refs):
    nb, steps, n_row, local_rows = cfg
    recv, out_ref, slots = refs[:n_row], refs[n_row], refs[n_row + 1]
    my_row = lax.axis_index("prow")
    slots[...] = jnp.zeros_like(slots)
    for k in range(n_row):
        slots[k * MOVE_SLOTS : k * MOVE_SLOTS + MOVE_ROWS, :] = recv[k][...]
    target = target_ref[...]
    for k in range(local_rows // nb):
        rows = slice(k * nb, (k + 1) * nb)
        hit = iota((nb, n_row * MOVE_SLOTS), 0) + k * nb == target
        moved = dot(one_hot(hit), slots[...]).astype(BF16)
        any_hit = jnp.sum(jnp.where(hit, 1.0, 0.0), axis=1, keepdims=True) > 0.5
        if k == 0:
            value = jnp.where(any_hit, moved, head_ref[...])
            value = jnp.where(my_row < steps, top_ref[...], value)
        else:
            value = jnp.where(any_hit, moved, res_ref[(k - 1) * nb : k * nb, :])
        out_ref[rows, :] = value


def call(kernel, outs, ins, scratch=(), any_at=(), flops=None):
    vmem = pl.BlockSpec(memory_space=pltpu.VMEM)
    anywhere = pl.BlockSpec(memory_space=pl.ANY)
    scalars = pl.BlockSpec(memory_space=pltpu.SMEM)
    return pl.pallas_call(
        kernel,
        out_shape=outs,
        in_specs=[
            jax.tree.map(lambda _: anywhere if i in any_at else vmem, x) for i, x in enumerate(ins)
        ],
        out_specs=jax.tree.map(lambda x: scalars if x.shape == (1,) else vmem, outs),
        scratch_shapes=list(scratch),
        compiler_params=pltpu.CompilerParams(vmem_limit_bytes=VMEM_BYTES),
        cost_estimate=flops
        and pl.CostEstimate(flops=flops, bytes_accessed=1 << 22, transcendentals=0),
    )(*ins)


def shape(*dims, dtype=BF16):
    return jax.ShapeDtypeStruct(dims, dtype)


def local(matrix, pivots, lower_inverse, upper_inverse):
    row_blocks, nb, col_blocks, _ = matrix.shape
    steps = pivots.shape[0]
    n_row = lax.axis_size("prow")
    n_col = lax.axis_size("pcol")
    if steps != 4 or col_blocks != 2 or n_row < steps or n_col < 8 or n_col % 4:
        return stepwise(matrix, pivots, lower_inverse, upper_inverse)
    local_rows = row_blocks * nb
    cap = -(-(steps * nb // n_row + 64) // 16) * 16
    mat = jnp.transpose(matrix, (2, 0, 1, 3)).reshape(col_blocks, local_rows, nb)
    m0 = mat[0]

    def from_panels(value, mask):
        return lax.ppermute(value, "pcol", [(i, i ^ mask) for i in range(steps)])

    def swap_cores(value):
        return lax.ppermute(value, "pcol", [(i, i ^ 1) for i in range(n_col)])

    def panel_pair(own, beside, far, far_beside):
        return jnp.where(on_panel, own, far), jnp.where(on_panel, beside, far_beside)

    on_panel = lax.axis_index("pcol") < steps
    fours = range(4, n_col, 4)
    meta, pack0, pack1 = call(
        functools.partial(pick_kernel, (nb, steps, n_row, cap, local_rows)),
        (shape(16, nb, dtype=I32), shape(cap, nb), shape(cap, nb)),
        (pivots, mat),
    )
    late0, pack0 = lax.optimization_barrier((m0, pack0))
    raw_x = from_panels(m0, 2)
    raw_far = functools.reduce(jnp.add, [from_panels(late0, mask) for mask in fours])
    parts = [pack0] + [
        lax.ppermute(pack0, "prow", [(i, (i + k) % n_row) for i in range(n_row)])
        for k in range(1, n_row)
    ]
    parts[1], raw_x = lax.optimization_barrier((parts[1], raw_x))
    raw_far_x = lax.ppermute(raw_far, "pcol", [(i, i ^ 2) for i in range(steps, n_col)])
    top0, off = call(
        functools.partial(order_kernel, (nb, steps, n_row, cap)),
        (shape(steps * nb, nb), shape((steps - 1) * nb, nb)),
        (meta, tuple(parts)),
        scratch=(pltpu.VMEM((n_row * cap, nb), BF16),),
    )
    pack1, off = lax.optimization_barrier((pack1, off))
    off_x = from_panels(off, 2)
    off_far = functools.reduce(jnp.add, [from_panels(off, mask) for mask in fours])
    off_far_x = functools.reduce(jnp.add, [from_panels(off, mask + 2) for mask in fours])
    buf1 = lax.all_gather(pack1, "prow", tiled=True)
    buf1, off_far, off_x, off_far_x = lax.optimization_barrier((buf1, off_far, off_x, off_far_x))
    raw_0, raw_2 = panel_pair(m0, raw_x, raw_far, raw_far_x)
    off_0, off_2 = panel_pair(off, off_x, off_far, off_far_x)
    raws = (raw_0, swap_cores(raw_0), raw_2, swap_cores(raw_2))
    offs = (off_0, swap_cores(off_0), off_2, swap_cores(off_2))
    top1 = call(
        functools.partial(second_kernel, (nb, steps, cap)), shape(steps * nb, nb), (meta, buf1)
    )
    top_rows = steps * nb
    upper, head, top, send = call(
        functools.partial(corner_kernel, (nb, steps, n_row)),
        (
            shape(top_rows, top_rows + 2 * nb), shape(nb, 2 * nb), shape(nb, 2 * nb),
            shape(n_row, MOVE_ROWS, 2 * nb),
        ),
        (pivots, top0, top1, mat, raws, offs, lower_inverse, upper_inverse),
        scratch=(
            pltpu.VMEM((steps, nb, nb), BF16),
            pltpu.VMEM((steps, top_rows - nb, nb), BF16),
            pltpu.VMEM((top_rows + nb, top_rows), BF16),
            pltpu.VMEM((top_rows, nb), BF16),
            pltpu.VMEM((steps, nb, nb), BF16),
            pltpu.SemaphoreType.DMA,
        ),
        any_at=(6,),
    )
    recv = [send[0]] + [
        lax.ppermute(send[k], "prow", [(i, (i + k) % n_row) for i in range(n_row)])
        for k in range(1, n_row)
    ]

    below = local_rows - nb
    res, target, crowded = call(
        functools.partial(rows_kernel, (nb, steps, n_row, cap, local_rows)),
        (
            shape(below, 2 * nb), shape(1, n_row * MOVE_SLOTS, dtype=I32), shape(1, dtype=I32),
        ),
        (pivots, meta, mat, raws, upper, upper_inverse),
        scratch=(
            pltpu.VMEM((steps, below, nb), BF16),
            pltpu.VMEM((below, top_rows), BF16),
            pltpu.VMEM((16, nb), I32),
        ),
        flops=2 * below * top_rows * (top_rows + 2 * nb),
    )

    def finish():
        out = call(
            functools.partial(place_kernel, (nb, steps, n_row, local_rows)),
            shape(local_rows, 2 * nb),
            (target, head, res, top, *recv),
            scratch=(pltpu.VMEM((n_row * MOVE_SLOTS, 2 * nb), BF16),),
        )
        return out.reshape(matrix.shape)

    return lax.cond(
        crowded[0] > 0,
        lambda: stepwise(matrix, pivots, lower_inverse, upper_inverse),
        finish,
    )


def solution(mesh):
    placed = (P(None, "prow", None, "pcol"), P(), P(), P())
    return jax.shard_map(
        local, mesh=mesh, in_specs=placed, out_specs=P(None, "prow", None, "pcol"), check_vma=False
    )
```

```python
import functools

import jax
import jax.numpy as jnp
from jax import lax
from jax.experimental import pallas as pl
from jax.experimental.pallas import tpu as pltpu
from jax.sharding import PartitionSpec as P

BF16 = jnp.bfloat16
F32 = jnp.float32
I32 = jnp.int32
VMEM_BYTES = 24 * 1024 * 1024
MOVE_ROWS = 64
MOVE_SLOTS = 128


def ring_sum(value, axis):
    size = lax.axis_size(axis)

    def turn(_, carry):
        total, passing = carry
        passing = lax.ppermute(passing, axis, [(i, (i + 1) % size) for i in range(size)])
        return total + passing, passing

    return lax.fori_loop(1, size, turn, (value, value))[0]


def spread(value, axis, source):
    kept = jnp.where(lax.axis_index(axis) == source, value, 0).astype(value.dtype)
    return ring_sum(kept, axis)


def stepwise(matrix, pivots, lower_inverse, upper_inverse):
    row_blocks = matrix.shape[0]
    block_size = matrix.shape[1]
    col_blocks = matrix.shape[2]
    local_rows = row_blocks * block_size
    local_cols = col_blocks * block_size
    matrix_loc = matrix.reshape(local_rows, local_cols)
    row_count = lax.axis_size("prow")
    col_count = lax.axis_size("pcol")
    my_row = lax.axis_index("prow")
    my_col = lax.axis_index("pcol")
    row_iota = jnp.arange(local_rows, dtype=jnp.int32)
    col_iota = jnp.arange(local_cols, dtype=jnp.int32)
    global_row = (row_iota // block_size * row_count + my_row) * block_size + row_iota % block_size
    global_col = (col_iota // block_size * col_count + my_col) * block_size + col_iota % block_size
    for step_num in range(pivots.shape[0]):
        begin_at = step_num * block_size
        trail_at = begin_at + block_size
        diag_root = step_num % row_count
        diag_local = step_num // row_count * block_size
        panel_root = step_num % col_count
        panel_local = step_num // col_count * block_size
        targets = begin_at + jnp.arange(block_size, dtype=jnp.int32)
        chosen = pivots[step_num]
        chosen_block = chosen // block_size
        chosen_owner = chosen_block % row_count
        is_mine = chosen_owner == my_row
        chosen_local = chosen_block // row_count * block_size + chosen % block_size
        picked = jnp.take(matrix_loc, jnp.where(is_mine, chosen_local, 0), axis=0)
        picked = jnp.where(is_mine[:, None], picked, jnp.zeros_like(picked))
        diag_rows = matrix_loc[diag_local : diag_local + block_size]
        own_diag = jnp.where(my_row == diag_root, diag_rows, jnp.zeros_like(diag_rows))
        new_rows, old_diag = ring_sum(picked, "prow"), ring_sum(own_diag, "prow")
        moved_rows = is_mine & (chosen != targets)
        matrix_loc = matrix_loc.at[jnp.where(moved_rows, chosen_local, local_rows)].set(
            old_diag, mode="drop"
        )
        diag_after = matrix_loc[diag_local : diag_local + block_size]
        matrix_loc = matrix_loc.at[diag_local : diag_local + block_size].set(
            jnp.where(my_row == diag_root, new_rows, diag_after)
        )
        upper_full = jnp.dot(
            lower_inverse[step_num], new_rows, preferred_element_type=jnp.float32
        ).astype(jnp.bfloat16)
        col_live = global_col >= trail_at
        upper_use = jnp.where(col_live[None, :], upper_full, jnp.zeros_like(upper_full))
        panel_own = matrix_loc[:, panel_local : panel_local + block_size]
        received = spread(panel_own, "pcol", panel_root)
        left_full = jnp.dot(
            received, upper_inverse[step_num], preferred_element_type=jnp.float32
        ).astype(jnp.bfloat16)
        row_live = global_row >= trail_at
        left_use = jnp.where(row_live[:, None], left_full, jnp.zeros_like(left_full))
        matrix_loc = (
            matrix_loc.astype(jnp.float32)
            - jnp.dot(left_use, upper_use, preferred_element_type=jnp.float32)
        ).astype(jnp.bfloat16)
        panel_now = matrix_loc[:, panel_local : panel_local + block_size]
        panel_put = jnp.where(row_live[:, None] & (my_col == panel_root), left_full, panel_now)
        matrix_loc = matrix_loc.at[:, panel_local : panel_local + block_size].set(panel_put)
        diag_now = matrix_loc[diag_local : diag_local + block_size]
        diag_put = jnp.where(col_live[None, :] & (my_row == diag_root), upper_full, diag_now)
        matrix_loc = matrix_loc.at[diag_local : diag_local + block_size].set(diag_put)
    return matrix_loc.reshape(matrix.shape)


def iota(shape, dim):
    return lax.broadcasted_iota(I32, shape, dim)


def dot(a, b):
    return jnp.dot(a, b, preferred_element_type=F32)


def one_hot(hit):
    return jnp.where(hit, 1.0, 0.0).astype(BF16)


def to_col(row, size):
    eye = iota((size, size), 0) == iota((size, size), 1)
    return jnp.sum(jnp.where(eye, jnp.broadcast_to(row, (size, size)), 0), axis=1, keepdims=True)


def find(col, base, x, size):
    hit = col == x
    place = jnp.sum(jnp.where(hit, iota((size, size), 0) + (base + 1), 0), axis=0, keepdims=True)
    return jnp.where(place > 0, place - 1, x)


def look(col, base, x, size):
    hit = iota((size, size), 0) + base == x
    return jnp.sum(jnp.where(hit, col, 0), axis=0, keepdims=True)


def before(rows, size):
    tri = one_hot(iota((size, size), 0) < iota((size, size), 1))
    stacked = jnp.concatenate([one_hot(r) for r in rows], axis=0)
    counts = dot(stacked, tri)
    k = rows[0].shape[0]
    return [counts[i * k : (i + 1) * k] for i in range(len(rows))]


def pick_kernel(cfg, piv_ref, mat_ref, meta_ref, pack0_ref, pack1_ref):
    nb, steps, n_row, cap, local_rows = cfg
    my_row = lax.axis_index("prow")
    piv = [piv_ref[t : t + 1, :] for t in range(steps)]
    cols = [to_col(piv[t], nb) for t in range(steps - 1)]
    owners, places = [], []
    for t in range(steps):
        x = piv[t]
        for s in range(t - 1, -1, -1):
            x = find(cols[s], s * nb, x, nb)
        block = x // nb
        owners.append(block % n_row)
        places.append(block // n_row * nb + x % nb)
    lanes = -(-n_row // 8) * 8
    member = [iota((lanes, nb), 0) == w for w in owners]
    counts = before(member, nb)
    base = jnp.zeros((lanes, 1), F32)
    ranks = []
    for t in range(steps):
        ranks.append(
            jnp.sum(jnp.where(member[t], counts[t] + base, 0.0), axis=0, keepdims=True).astype(I32)
        )
        base = base + jnp.sum(jnp.where(member[t], 1.0, 0.0), axis=1, keepdims=True)
    for t in range(steps):
        meta_ref[t : t + 1, :] = owners[t]
        meta_ref[steps + t : steps + t + 1, :] = ranks[t]
    over = jnp.max(base, axis=0, keepdims=True).astype(I32)
    meta_ref[2 * steps : 2 * steps + 1, :] = jnp.broadcast_to(over, (1, nb))
    slot = iota((cap, nb), 0)
    total = jnp.zeros((cap, nb), I32)
    for t in range(steps):
        key = jnp.where(owners[t] == my_row, ranks[t], -1)
        total = total + jnp.where(slot == key, places[t] + 1, 0)
    source = jnp.sum(total, axis=1, keepdims=True) - 1
    chosen = one_hot(source == iota((cap, local_rows), 1))
    pack0_ref[...] = dot(chosen, mat_ref[0]).astype(BF16)
    pack1_ref[...] = dot(chosen, mat_ref[1]).astype(BF16)


def final_places(x, piv_ref, cols, steps, size):
    for s in range(steps):
        base = s * size
        inside = (x >= base) & (x < base + size)
        x = jnp.where(inside, look(cols[s], base, x, size), find(cols[s], base, x, size))
    return x


def find_moves(cfg, piv_ref, meta_ref, move_ref):
    nb, steps, n_row, cap = cfg
    cols = [to_col(piv_ref[t : t + 1, :], nb) for t in range(steps)]
    lanes = -(-n_row // 8) * 8
    member = []
    for t in range(steps):
        x = final_places(iota((1, nb), 1) + t * nb, piv_ref, cols, steps, nb)
        block = x // nb
        dest = jnp.where(x >= steps * nb, block % n_row, -1)
        move_ref[t : t + 1, :] = dest
        move_ref[2 * steps + t : 2 * steps + t + 1, :] = block // n_row * nb + x % nb
        member.append(iota((lanes, nb), 0) == dest)
    counts = before(member, nb)
    most = jnp.zeros((lanes, 1), F32)
    for t in range(steps):
        move_ref[steps + t : steps + t + 1, :] = jnp.sum(
            jnp.where(member[t], counts[t], 0.0), axis=0, keepdims=True
        ).astype(I32)
        most = jnp.maximum(most, jnp.sum(jnp.where(member[t], 1.0, 0.0), axis=1, keepdims=True))
    over = jnp.max(most, axis=0, keepdims=True).astype(I32)
    bad = (over > MOVE_ROWS) | (meta_ref[2 * steps : 2 * steps + 1, :] > cap)
    return jnp.where(bad, 1, 0)


def find_targets(cfg, move_ref, my_row):
    nb, steps, n_row = cfg
    targets = []
    for k in range(n_row):
        here = iota((steps, nb), 0) == lax.rem(my_row + n_row - k, n_row)
        dest = jnp.sum(jnp.where(here, move_ref[:steps, :] + 1, 0), axis=0, keepdims=True) - 1
        rank = jnp.sum(jnp.where(here, move_ref[steps : 2 * steps, :], 0), axis=0, keepdims=True)
        place = jnp.sum(
            jnp.where(here, move_ref[2 * steps : 3 * steps, :], 0), axis=0, keepdims=True
        )
        key = jnp.where(dest == my_row, rank, -1)
        hot = one_hot(key == iota((MOVE_SLOTS, nb), 0))
        row = iota((8, nb), 0)
        parts = jnp.where(row == 0, place // 128, jnp.where(row == 1, place % 128, 1))
        found = lax.dot_general(
            parts.astype(F32).astype(BF16), hot, (((1,), (1,)), ((), ())),
            preferred_element_type=F32,
        )
        at = found[0:1] * 128.0 + found[1:2]
        targets.append(jnp.where(found[2:3] > 0.5, at, -1.0).astype(I32))
    return jnp.concatenate(targets, axis=1)


def order_rows(pos, buf_ref):
    nb = pos.shape[1]
    hot = one_hot(to_col(pos, nb) == iota((nb, buf_ref.shape[0]), 1))
    return dot(hot, buf_ref[...]).astype(BF16)


def order_kernel(cfg, meta_ref, parts, top_ref, off_ref, buf):
    nb, steps, n_row, cap = cfg
    my_row = lax.axis_index("prow")
    my_col = lax.axis_index("pcol")
    for k in range(n_row):
        buf[k * cap : (k + 1) * cap, :] = parts[k][...]
    for t in range(steps):
        turn = my_row - meta_ref[t : t + 1, :]
        turn = jnp.where(turn < 0, turn + n_row, turn)
        pos = turn * cap + meta_ref[steps + t : steps + t + 1, :]
        top_ref[t * nb : (t + 1) * nb, :] = order_rows(pos, buf)
    for j in range(steps - 1):
        block = jnp.where(my_col <= j, j + 1, j)
        rows = pl.ds(pl.multiple_of(block * nb, nb), nb)
        off_ref[j * nb : (j + 1) * nb, :] = top_ref[rows, :]


def second_kernel(cfg, meta_ref, buf_ref, top_ref):
    nb, steps, cap = cfg
    for t in range(steps):
        pos = meta_ref[t : t + 1, :] * cap + meta_ref[steps + t : steps + t + 1, :]
        top_ref[t * nb : (t + 1) * nb, :] = order_rows(pos, buf_ref)


def sort_panels(panels, into, rows):
    low = lax.axis_index("pcol") & 3
    for mask, panel in enumerate(panels):
        into[low ^ mask] = panel[rows, :]


def corner_kernel(
    cfg, piv_ref, top0_ref, top1_ref, mat_ref, raws, offs, linv_hbm, uinv_ref,
    upper, res_ref, top_ref, send_ref, raw, off, left, diag, linv_ref, sem,
):
    nb, steps, n_row = cfg
    wide = steps * nb
    my_row = lax.axis_index("prow")
    my_col = lax.axis_index("pcol")
    load = pltpu.make_async_copy(linv_hbm, linv_ref, sem)
    load.start()
    sort_panels(offs, off, slice(0, wide - nb))
    sort_panels(raws, raw, slice(0, nb))
    load.wait()
    for t in range(steps):
        here = slice(t * nb, (t + 1) * nb)
        done = slice(0, t * nb)
        parts = [off[j, here, :] for j in range(t + 1, steps)]
        parts += [top0_ref[here, :], top1_ref[here, :]]
        column = [off[t, t * nb :, :]] if t < steps - 1 else []
        column += [raw[t]]
        if t > 0:
            prod = dot(left[here, done], upper[done, (t + 1) * nb :])
            parts = [
                (p.astype(F32) - prod[:, i * nb : (i + 1) * nb]).astype(BF16)
                for i, p in enumerate(parts)
            ]
            prod = dot(left[(t + 1) * nb :, done], upper[done, here])
            at = 0
            for i, p in enumerate(column):
                rows = p.shape[0]
                column[i] = (p.astype(F32) - prod[at : at + rows]).astype(BF16)
                at += rows
        diag[here, :] = parts[-2]
        upper[here, (t + 1) * nb :] = dot(linv_ref[t], jnp.concatenate(parts, axis=1)).astype(BF16)
        left[(t + 1) * nb :, here] = dot(jnp.concatenate(column, axis=0), uinv_ref[t]).astype(BF16)
    in_panel = my_col < steps
    panel = pl.ds(pl.multiple_of(jnp.minimum(my_col, steps - 1) * nb, nb), nb)
    prod = dot(left[wide:, :], upper[:, wide:])
    value = (mat_ref[0, :nb, :].astype(F32) - prod[:, :nb]).astype(BF16)
    res_ref[:, :nb] = jnp.where(in_panel, left[wide:, panel], value)
    res_ref[:, nb:] = (mat_ref[1, :nb, :].astype(F32) - prod[:, nb:]).astype(BF16)
    cols = [to_col(piv_ref[t : t + 1, :], nb) for t in range(steps)]
    x = final_places(iota((1, nb), 1) + my_row * nb, piv_ref, cols, steps, nb)
    dest = jnp.where((x >= wide) & (my_row < steps), x // nb % n_row, -1)
    member = iota((-(-n_row // 8) * 8, nb), 0) == dest
    rank = jnp.sum(jnp.where(member, before([member], nb)[0], 0.0), axis=0, keepdims=True)
    rank = rank.astype(I32)
    hot = []
    for k in range(n_row):
        key = jnp.where(dest == lax.rem(my_row + k, n_row), rank, -1)
        hot.append(one_hot(key == iota((MOVE_ROWS, nb), 0)))
    moved = dot(jnp.concatenate(hot, axis=0), res_ref[...]).astype(BF16)
    for k in range(n_row):
        send_ref[k] = moved[k * MOVE_ROWS : (k + 1) * MOVE_ROWS]
    block = pl.ds(pl.multiple_of(jnp.minimum(my_row, steps - 1) * nb, nb), nb)
    value = jnp.where(my_col == my_row, diag[block, :], upper[block, wide : wide + nb])
    value = jnp.where(in_panel & (my_col < my_row), left[block, panel], value)
    top_ref[:, :nb] = value
    top_ref[:, nb:] = upper[block, wide + nb :]


def rows_kernel(
    cfg, piv_ref, meta_ref, mat_ref, raws, upper, uinv_ref, res_ref, target_ref,
    flag_ref, raw, l_own, move_ref,
):
    nb, steps, n_row, cap, local_rows = cfg
    my_col = lax.axis_index("pcol")
    sort_panels(raws, raw, slice(nb, local_rows))
    bad = find_moves((nb, steps, n_row, cap), piv_ref, meta_ref, move_ref)
    target_ref[...] = find_targets((nb, steps, n_row), move_ref, lax.axis_index("prow"))
    flag_ref[0] = jnp.max(bad)
    tiles = [slice(k * nb, (k + 1) * nb) for k in range(local_rows // nb - 1)]
    for t in range(steps):
        here = slice(t * nb, (t + 1) * nb)
        done = slice(0, t * nb)
        for rows in tiles:
            acc = raw[t, rows, :].astype(F32)
            if t > 0:
                acc = acc - dot(l_own[rows, done], upper[done, here])
            l_own[rows, here] = dot(acc.astype(BF16), uinv_ref[t]).astype(BF16)
    in_panel = my_col < steps
    panel = pl.ds(pl.multiple_of(jnp.minimum(my_col, steps - 1) * nb, nb), nb)
    for rows in tiles:
        prod = dot(l_own[rows, :], upper[:, steps * nb :])
        source = slice(rows.start + nb, rows.stop + nb)
        left = (mat_ref[0, source, :].astype(F32) - prod[:, :nb]).astype(BF16)
        res_ref[rows, :nb] = jnp.where(in_panel, l_own[rows, panel], left)
        res_ref[rows, nb:] = (mat_ref[1, source, :].astype(F32) - prod[:, nb:]).astype(BF16)


def place_kernel(cfg, target_ref, head_ref, res_ref, top_ref, *refs):
    nb, steps, n_row, local_rows = cfg
    recv, out_ref, slots = refs[:n_row], refs[n_row], refs[n_row + 1]
    my_row = lax.axis_index("prow")
    slots[...] = jnp.zeros_like(slots)
    for k in range(n_row):
        slots[k * MOVE_SLOTS : k * MOVE_SLOTS + MOVE_ROWS, :] = recv[k][...]
    target = target_ref[...]
    for k in range(local_rows // nb):
        rows = slice(k * nb, (k + 1) * nb)
        hit = iota((nb, n_row * MOVE_SLOTS), 0) + k * nb == target
        moved = dot(one_hot(hit), slots[...]).astype(BF16)
        any_hit = jnp.sum(jnp.where(hit, 1.0, 0.0), axis=1, keepdims=True) > 0.5
        if k == 0:
            value = jnp.where(any_hit, moved, head_ref[...])
            value = jnp.where(my_row < steps, top_ref[...], value)
        else:
            value = jnp.where(any_hit, moved, res_ref[(k - 1) * nb : k * nb, :])
        out_ref[rows, :] = value


def call(kernel, outs, ins, scratch=(), any_at=(), flops=None):
    vmem = pl.BlockSpec(memory_space=pltpu.VMEM)
    anywhere = pl.BlockSpec(memory_space=pl.ANY)
    scalars = pl.BlockSpec(memory_space=pltpu.SMEM)
    return pl.pallas_call(
        kernel,
        out_shape=outs,
        in_specs=[
            jax.tree.map(lambda _: anywhere if i in any_at else vmem, x) for i, x in enumerate(ins)
        ],
        out_specs=jax.tree.map(lambda x: scalars if x.shape == (1,) else vmem, outs),
        scratch_shapes=list(scratch),
        compiler_params=pltpu.CompilerParams(vmem_limit_bytes=VMEM_BYTES),
        cost_estimate=flops
        and pl.CostEstimate(flops=flops, bytes_accessed=1 << 22, transcendentals=0),
    )(*ins)


def shape(*dims, dtype=BF16):
    return jax.ShapeDtypeStruct(dims, dtype)


def local(matrix, pivots, lower_inverse, upper_inverse):
    row_blocks, nb, col_blocks, _ = matrix.shape
    steps = pivots.shape[0]
    n_row = lax.axis_size("prow")
    n_col = lax.axis_size("pcol")
    if steps != 4 or col_blocks != 2 or n_row < steps or n_col < 8 or n_col % 4:
        return stepwise(matrix, pivots, lower_inverse, upper_inverse)
    local_rows = row_blocks * nb
    cap = -(-(steps * nb // n_row + 48) // 16) * 16
    mat = jnp.transpose(matrix, (2, 0, 1, 3)).reshape(col_blocks, local_rows, nb)
    m0 = mat[0]

    def from_panels(value, mask):
        return lax.ppermute(value, "pcol", [(i, i ^ mask) for i in range(steps)])

    def swap_cores(value):
        return lax.ppermute(value, "pcol", [(i, i ^ 1) for i in range(n_col)])

    def panel_pair(own, beside, far, far_beside):
        return jnp.where(on_panel, own, far), jnp.where(on_panel, beside, far_beside)

    on_panel = lax.axis_index("pcol") < steps
    fours = range(4, n_col, 4)
    meta, pack0, pack1 = call(
        functools.partial(pick_kernel, (nb, steps, n_row, cap, local_rows)),
        (shape(16, nb, dtype=I32), shape(cap, nb), shape(cap, nb)),
        (pivots, mat),
    )
    late0, pack0 = lax.optimization_barrier((m0, pack0))
    raw_x = from_panels(m0, 2)
    raw_far = functools.reduce(jnp.add, [from_panels(late0, mask) for mask in fours])
    parts = [pack0] + [
        lax.ppermute(pack0, "prow", [(i, (i + k) % n_row) for i in range(n_row)])
        for k in range(1, n_row)
    ]
    parts[1], raw_x = lax.optimization_barrier((parts[1], raw_x))
    raw_far_x = lax.ppermute(raw_far, "pcol", [(i, i ^ 2) for i in range(steps, n_col)])
    top0, off = call(
        functools.partial(order_kernel, (nb, steps, n_row, cap)),
        (shape(steps * nb, nb), shape((steps - 1) * nb, nb)),
        (meta, tuple(parts)),
        scratch=(pltpu.VMEM((n_row * cap, nb), BF16),),
    )
    pack1, off = lax.optimization_barrier((pack1, off))
    off_far = functools.reduce(jnp.add, [from_panels(off, mask) for mask in fours])
    off_x = from_panels(off, 2)
    off_far_x = functools.reduce(jnp.add, [from_panels(off, mask + 2) for mask in fours])
    buf1 = lax.all_gather(pack1, "prow", tiled=True)
    buf1, off_x, off_far_x, off_far = lax.optimization_barrier((buf1, off_x, off_far_x, off_far))
    raw_0, raw_2 = panel_pair(m0, raw_x, raw_far, raw_far_x)
    off_0, off_2 = panel_pair(off, off_x, off_far, off_far_x)
    raws = (raw_0, swap_cores(raw_0), raw_2, swap_cores(raw_2))
    offs = (off_0, swap_cores(off_0), off_2, swap_cores(off_2))
    top1 = call(
        functools.partial(second_kernel, (nb, steps, cap)), shape(steps * nb, nb), (meta, buf1)
    )
    top_rows = steps * nb
    upper, head, top, send = call(
        functools.partial(corner_kernel, (nb, steps, n_row)),
        (
            shape(top_rows, top_rows + 2 * nb), shape(nb, 2 * nb), shape(nb, 2 * nb),
            shape(n_row, MOVE_ROWS, 2 * nb),
        ),
        (pivots, top0, top1, mat, raws, offs, lower_inverse, upper_inverse),
        scratch=(
            pltpu.VMEM((steps, nb, nb), BF16),
            pltpu.VMEM((steps, top_rows - nb, nb), BF16),
            pltpu.VMEM((top_rows + nb, top_rows), BF16),
            pltpu.VMEM((top_rows, nb), BF16),
            pltpu.VMEM((steps, nb, nb), BF16),
            pltpu.SemaphoreType.DMA,
        ),
        any_at=(6,),
    )
    recv = [send[0]] + [
        lax.ppermute(send[k], "prow", [(i, (i + k) % n_row) for i in range(n_row)])
        for k in range(1, n_row)
    ]

    below = local_rows - nb
    res, target, crowded = call(
        functools.partial(rows_kernel, (nb, steps, n_row, cap, local_rows)),
        (
            shape(below, 2 * nb), shape(1, n_row * MOVE_SLOTS, dtype=I32), shape(1, dtype=I32),
        ),
        (pivots, meta, mat, raws, upper, upper_inverse),
        scratch=(
            pltpu.VMEM((steps, below, nb), BF16),
            pltpu.VMEM((below, top_rows), BF16),
            pltpu.VMEM((16, nb), I32),
        ),
        flops=2 * below * top_rows * (top_rows + 2 * nb),
    )

    def finish():
        out = call(
            functools.partial(place_kernel, (nb, steps, n_row, local_rows)),
            shape(local_rows, 2 * nb),
            (target, head, res, top, *recv),
            scratch=(pltpu.VMEM((n_row * MOVE_SLOTS, 2 * nb), BF16),),
        )
        return out.reshape(matrix.shape)

    return lax.cond(
        crowded[0] > 0,
        lambda: stepwise(matrix, pivots, lower_inverse, upper_inverse),
        finish,
    )


def solution(mesh):
    placed = (P(None, "prow", None, "pcol"), P(), P(), P())
    return jax.shard_map(
        local, mesh=mesh, in_specs=placed, out_specs=P(None, "prow", None, "pcol"), check_vma=False
    )
```

```python
import functools

import jax
import jax.numpy as jnp
from jax import lax
from jax.experimental import pallas as pl
from jax.experimental.pallas import tpu as pltpu
from jax.sharding import PartitionSpec as P

BF16 = jnp.bfloat16
F32 = jnp.float32
I32 = jnp.int32
VMEM_BYTES = 24 * 1024 * 1024
MOVE_ROWS = 64
MOVE_SLOTS = 128


def ring_sum(value, axis):
    size = lax.axis_size(axis)

    def turn(_, carry):
        total, passing = carry
        passing = lax.ppermute(passing, axis, [(i, (i + 1) % size) for i in range(size)])
        return total + passing, passing

    return lax.fori_loop(1, size, turn, (value, value))[0]


def spread(value, axis, source):
    kept = jnp.where(lax.axis_index(axis) == source, value, 0).astype(value.dtype)
    return ring_sum(kept, axis)


def stepwise(matrix, pivots, lower_inverse, upper_inverse):
    row_blocks = matrix.shape[0]
    block_size = matrix.shape[1]
    col_blocks = matrix.shape[2]
    local_rows = row_blocks * block_size
    local_cols = col_blocks * block_size
    matrix_loc = matrix.reshape(local_rows, local_cols)
    row_count = lax.axis_size("prow")
    col_count = lax.axis_size("pcol")
    my_row = lax.axis_index("prow")
    my_col = lax.axis_index("pcol")
    row_iota = jnp.arange(local_rows, dtype=jnp.int32)
    col_iota = jnp.arange(local_cols, dtype=jnp.int32)
    global_row = (row_iota // block_size * row_count + my_row) * block_size + row_iota % block_size
    global_col = (col_iota // block_size * col_count + my_col) * block_size + col_iota % block_size
    for step_num in range(pivots.shape[0]):
        begin_at = step_num * block_size
        trail_at = begin_at + block_size
        diag_root = step_num % row_count
        diag_local = step_num // row_count * block_size
        panel_root = step_num % col_count
        panel_local = step_num // col_count * block_size
        targets = begin_at + jnp.arange(block_size, dtype=jnp.int32)
        chosen = pivots[step_num]
        chosen_block = chosen // block_size
        chosen_owner = chosen_block % row_count
        is_mine = chosen_owner == my_row
        chosen_local = chosen_block // row_count * block_size + chosen % block_size
        picked = jnp.take(matrix_loc, jnp.where(is_mine, chosen_local, 0), axis=0)
        picked = jnp.where(is_mine[:, None], picked, jnp.zeros_like(picked))
        diag_rows = matrix_loc[diag_local : diag_local + block_size]
        own_diag = jnp.where(my_row == diag_root, diag_rows, jnp.zeros_like(diag_rows))
        new_rows, old_diag = ring_sum(picked, "prow"), ring_sum(own_diag, "prow")
        moved_rows = is_mine & (chosen != targets)
        matrix_loc = matrix_loc.at[jnp.where(moved_rows, chosen_local, local_rows)].set(
            old_diag, mode="drop"
        )
        diag_after = matrix_loc[diag_local : diag_local + block_size]
        matrix_loc = matrix_loc.at[diag_local : diag_local + block_size].set(
            jnp.where(my_row == diag_root, new_rows, diag_after)
        )
        upper_full = jnp.dot(
            lower_inverse[step_num], new_rows, preferred_element_type=jnp.float32
        ).astype(jnp.bfloat16)
        col_live = global_col >= trail_at
        upper_use = jnp.where(col_live[None, :], upper_full, jnp.zeros_like(upper_full))
        panel_own = matrix_loc[:, panel_local : panel_local + block_size]
        received = spread(panel_own, "pcol", panel_root)
        left_full = jnp.dot(
            received, upper_inverse[step_num], preferred_element_type=jnp.float32
        ).astype(jnp.bfloat16)
        row_live = global_row >= trail_at
        left_use = jnp.where(row_live[:, None], left_full, jnp.zeros_like(left_full))
        matrix_loc = (
            matrix_loc.astype(jnp.float32)
            - jnp.dot(left_use, upper_use, preferred_element_type=jnp.float32)
        ).astype(jnp.bfloat16)
        panel_now = matrix_loc[:, panel_local : panel_local + block_size]
        panel_put = jnp.where(row_live[:, None] & (my_col == panel_root), left_full, panel_now)
        matrix_loc = matrix_loc.at[:, panel_local : panel_local + block_size].set(panel_put)
        diag_now = matrix_loc[diag_local : diag_local + block_size]
        diag_put = jnp.where(col_live[None, :] & (my_row == diag_root), upper_full, diag_now)
        matrix_loc = matrix_loc.at[diag_local : diag_local + block_size].set(diag_put)
    return matrix_loc.reshape(matrix.shape)


def iota(shape, dim):
    return lax.broadcasted_iota(I32, shape, dim)


def dot(a, b):
    return jnp.dot(a, b, preferred_element_type=F32)


def one_hot(hit):
    return jnp.where(hit, 1.0, 0.0).astype(BF16)


def to_col(row, size):
    eye = iota((size, size), 0) == iota((size, size), 1)
    return jnp.sum(jnp.where(eye, jnp.broadcast_to(row, (size, size)), 0), axis=1, keepdims=True)


def find(col, base, x, size):
    hit = col == x
    place = jnp.sum(jnp.where(hit, iota((size, size), 0) + (base + 1), 0), axis=0, keepdims=True)
    return jnp.where(place > 0, place - 1, x)


def look(col, base, x, size):
    hit = iota((size, size), 0) + base == x
    return jnp.sum(jnp.where(hit, col, 0), axis=0, keepdims=True)


def before(rows, size):
    tri = one_hot(iota((size, size), 0) < iota((size, size), 1))
    stacked = jnp.concatenate([one_hot(r) for r in rows], axis=0)
    counts = dot(stacked, tri)
    k = rows[0].shape[0]
    return [counts[i * k : (i + 1) * k] for i in range(len(rows))]


def pick_kernel(cfg, piv_ref, mat_ref, meta_ref, pack0_ref, pack1_ref):
    nb, steps, n_row, cap, local_rows = cfg
    my_row = lax.axis_index("prow")
    piv = [piv_ref[t : t + 1, :] for t in range(steps)]
    cols = [to_col(piv[t], nb) for t in range(steps - 1)]
    owners, places = [], []
    for t in range(steps):
        x = piv[t]
        for s in range(t - 1, -1, -1):
            x = find(cols[s], s * nb, x, nb)
        block = x // nb
        owners.append(block % n_row)
        places.append(block // n_row * nb + x % nb)
    lanes = -(-n_row // 8) * 8
    member = [iota((lanes, nb), 0) == w for w in owners]
    counts = before(member, nb)
    base = jnp.zeros((lanes, 1), F32)
    ranks = []
    for t in range(steps):
        ranks.append(
            jnp.sum(jnp.where(member[t], counts[t] + base, 0.0), axis=0, keepdims=True).astype(I32)
        )
        base = base + jnp.sum(jnp.where(member[t], 1.0, 0.0), axis=1, keepdims=True)
    for t in range(steps):
        meta_ref[t : t + 1, :] = owners[t]
        meta_ref[steps + t : steps + t + 1, :] = ranks[t]
    over = jnp.max(base, axis=0, keepdims=True).astype(I32)
    meta_ref[2 * steps : 2 * steps + 1, :] = jnp.broadcast_to(over, (1, nb))
    slot = iota((cap, nb), 0)
    total = jnp.zeros((cap, nb), I32)
    for t in range(steps):
        key = jnp.where(owners[t] == my_row, ranks[t], -1)
        total = total + jnp.where(slot == key, places[t] + 1, 0)
    source = jnp.sum(total, axis=1, keepdims=True) - 1
    chosen = one_hot(source == iota((cap, local_rows), 1))
    pack0_ref[...] = dot(chosen, mat_ref[0]).astype(BF16)
    pack1_ref[...] = dot(chosen, mat_ref[1]).astype(BF16)


def final_places(x, cols, steps, size):
    for s in steps:
        base = s * size
        inside = (x >= base) & (x < base + size)
        x = jnp.where(inside, look(cols[s], base, x, size), find(cols[s], base, x, size))
    return x


def find_moves(cfg, piv_ref, meta_ref, move_ref):
    nb, steps, n_row, cap = cfg
    cols = [to_col(piv_ref[t : t + 1, :], nb) for t in range(steps)]
    lanes = -(-n_row // 8) * 8
    member = []
    for t in range(steps):
        at = iota((1, nb), 1) + t * nb
        x = at
        for s in range(t):
            x = find(cols[s], s * nb, x, nb)
        x = jnp.where(x == at, piv_ref[t : t + 1, :], x)
        x = final_places(x, cols, range(t + 1, steps), nb)
        block = x // nb
        dest = jnp.where(x >= steps * nb, block % n_row, -1)
        move_ref[t : t + 1, :] = dest
        move_ref[2 * steps + t : 2 * steps + t + 1, :] = block // n_row * nb + x % nb
        member.append(iota((lanes, nb), 0) == dest)
    counts = before(member, nb)
    most = jnp.zeros((lanes, 1), F32)
    for t in range(steps):
        move_ref[steps + t : steps + t + 1, :] = jnp.sum(
            jnp.where(member[t], counts[t], 0.0), axis=0, keepdims=True
        ).astype(I32)
        most = jnp.maximum(most, jnp.sum(jnp.where(member[t], 1.0, 0.0), axis=1, keepdims=True))
    over = jnp.max(most, axis=0, keepdims=True).astype(I32)
    bad = (over > MOVE_ROWS) | (meta_ref[2 * steps : 2 * steps + 1, :] > cap)
    return jnp.where(bad, 1, 0)


def find_targets(cfg, move_ref, my_row):
    nb, steps, n_row = cfg
    targets = []
    for k in range(n_row):
        here = iota((steps, nb), 0) == lax.rem(my_row + n_row - k, n_row)
        dest = jnp.sum(jnp.where(here, move_ref[:steps, :] + 1, 0), axis=0, keepdims=True) - 1
        rank = jnp.sum(jnp.where(here, move_ref[steps : 2 * steps, :], 0), axis=0, keepdims=True)
        place = jnp.sum(
            jnp.where(here, move_ref[2 * steps : 3 * steps, :], 0), axis=0, keepdims=True
        )
        key = jnp.where(dest == my_row, rank, -1)
        hot = one_hot(key == iota((MOVE_SLOTS, nb), 0))
        row = iota((8, nb), 0)
        parts = jnp.where(row == 0, place // 128, jnp.where(row == 1, place % 128, 1))
        found = lax.dot_general(
            parts.astype(F32).astype(BF16), hot, (((1,), (1,)), ((), ())),
            preferred_element_type=F32,
        )
        at = found[0:1] * 128.0 + found[1:2]
        targets.append(jnp.where(found[2:3] > 0.5, at, -1.0).astype(I32))
    return jnp.concatenate(targets, axis=1)


def order_rows(pos, buf_ref):
    nb = pos.shape[1]
    hot = one_hot(to_col(pos, nb) == iota((nb, buf_ref.shape[0]), 1))
    return dot(hot, buf_ref[...]).astype(BF16)


def order_kernel(cfg, meta_ref, parts, top_ref, off_ref, buf):
    nb, steps, n_row, cap = cfg
    my_row = lax.axis_index("prow")
    my_col = lax.axis_index("pcol")
    for k in range(n_row):
        buf[k * cap : (k + 1) * cap, :] = parts[k][...]
    for t in range(steps):
        turn = my_row - meta_ref[t : t + 1, :]
        turn = jnp.where(turn < 0, turn + n_row, turn)
        pos = turn * cap + meta_ref[steps + t : steps + t + 1, :]
        top_ref[t * nb : (t + 1) * nb, :] = order_rows(pos, buf)
    for j in range(steps - 1):
        block = jnp.where(my_col <= j, j + 1, j)
        rows = pl.ds(pl.multiple_of(block * nb, nb), nb)
        off_ref[j * nb : (j + 1) * nb, :] = top_ref[rows, :]


def second_kernel(cfg, meta_ref, buf_ref, top_ref):
    nb, steps, cap = cfg
    for t in range(steps):
        pos = meta_ref[t : t + 1, :] * cap + meta_ref[steps + t : steps + t + 1, :]
        top_ref[t * nb : (t + 1) * nb, :] = order_rows(pos, buf_ref)


def sort_panels(panels, into, rows):
    low = lax.axis_index("pcol") & 3
    for mask, panel in enumerate(panels):
        into[low ^ mask] = panel[rows, :]


def corner_kernel(
    cfg, piv_ref, top0_ref, top1_ref, mat_ref, raws, offs, linv_hbm, uinv_ref,
    upper, res_ref, top_ref, send_ref, raw, off, left, diag, linv_ref, sem,
):
    nb, steps, n_row = cfg
    wide = steps * nb
    my_row = lax.axis_index("prow")
    my_col = lax.axis_index("pcol")
    load = pltpu.make_async_copy(linv_hbm, linv_ref, sem)
    load.start()
    sort_panels(offs, off, slice(0, wide - nb))
    sort_panels(raws, raw, slice(0, nb))
    load.wait()
    for t in range(steps):
        here = slice(t * nb, (t + 1) * nb)
        done = slice(0, t * nb)
        parts = [off[j, here, :] for j in range(t + 1, steps)]
        parts += [top0_ref[here, :], top1_ref[here, :]]
        column = [off[t, t * nb :, :]] if t < steps - 1 else []
        column += [raw[t]]
        if t > 0:
            prod = dot(left[here, done], upper[done, (t + 1) * nb :])
            parts = [
                (p.astype(F32) - prod[:, i * nb : (i + 1) * nb]).astype(BF16)
                for i, p in enumerate(parts)
            ]
            prod = dot(left[(t + 1) * nb :, done], upper[done, here])
            at = 0
            for i, p in enumerate(column):
                rows = p.shape[0]
                column[i] = (p.astype(F32) - prod[at : at + rows]).astype(BF16)
                at += rows
        diag[here, :] = parts[-2]
        upper[here, (t + 1) * nb :] = dot(linv_ref[t], jnp.concatenate(parts, axis=1)).astype(BF16)
        left[(t + 1) * nb :, here] = dot(jnp.concatenate(column, axis=0), uinv_ref[t]).astype(BF16)
    in_panel = my_col < steps
    panel = pl.ds(pl.multiple_of(jnp.minimum(my_col, steps - 1) * nb, nb), nb)
    prod = dot(left[wide:, :], upper[:, wide:])
    value = (mat_ref[0, :nb, :].astype(F32) - prod[:, :nb]).astype(BF16)
    res_ref[:, :nb] = jnp.where(in_panel, left[wide:, panel], value)
    res_ref[:, nb:] = (mat_ref[1, :nb, :].astype(F32) - prod[:, nb:]).astype(BF16)
    cols = [to_col(piv_ref[t : t + 1, :], nb) for t in range(steps)]
    x = final_places(iota((1, nb), 1) + my_row * nb, cols, range(steps), nb)
    dest = jnp.where((x >= wide) & (my_row < steps), x // nb % n_row, -1)
    member = iota((-(-n_row // 8) * 8, nb), 0) == dest
    rank = jnp.sum(jnp.where(member, before([member], nb)[0], 0.0), axis=0, keepdims=True)
    rank = rank.astype(I32)
    hot = []
    for k in range(n_row):
        key = jnp.where(dest == lax.rem(my_row + k, n_row), rank, -1)
        hot.append(one_hot(key == iota((MOVE_ROWS, nb), 0)))
    moved = dot(jnp.concatenate(hot, axis=0), res_ref[...]).astype(BF16)
    for k in range(n_row):
        send_ref[k] = moved[k * MOVE_ROWS : (k + 1) * MOVE_ROWS]
    block = pl.ds(pl.multiple_of(jnp.minimum(my_row, steps - 1) * nb, nb), nb)
    value = jnp.where(my_col == my_row, diag[block, :], upper[block, wide : wide + nb])
    value = jnp.where(in_panel & (my_col < my_row), left[block, panel], value)
    top_ref[:, :nb] = value
    top_ref[:, nb:] = upper[block, wide + nb :]


def rows_kernel(
    cfg, piv_ref, meta_ref, mat_ref, raws, upper, uinv_ref, res_ref, target_ref,
    flag_ref, raw, l_own, move_ref,
):
    nb, steps, n_row, cap, local_rows = cfg
    my_col = lax.axis_index("pcol")
    sort_panels(raws, raw, slice(nb, local_rows))
    bad = find_moves((nb, steps, n_row, cap), piv_ref, meta_ref, move_ref)
    target_ref[...] = find_targets((nb, steps, n_row), move_ref, lax.axis_index("prow"))
    flag_ref[0] = jnp.max(bad)
    tiles = [slice(0, local_rows - nb)]
    for t in range(steps):
        here = slice(t * nb, (t + 1) * nb)
        done = slice(0, t * nb)
        for rows in tiles:
            acc = raw[t, rows, :].astype(F32)
            if t > 0:
                acc = acc - dot(l_own[rows, done], upper[done, here])
            l_own[rows, here] = dot(acc.astype(BF16), uinv_ref[t]).astype(BF16)
    in_panel = my_col < steps
    panel = pl.ds(pl.multiple_of(jnp.minimum(my_col, steps - 1) * nb, nb), nb)
    for rows in tiles:
        prod = dot(l_own[rows, :], upper[:, steps * nb :])
        source = slice(rows.start + nb, rows.stop + nb)
        left = (mat_ref[0, source, :].astype(F32) - prod[:, :nb]).astype(BF16)
        res_ref[rows, :nb] = jnp.where(in_panel, l_own[rows, panel], left)
        res_ref[rows, nb:] = (mat_ref[1, source, :].astype(F32) - prod[:, nb:]).astype(BF16)


def place_kernel(cfg, target_ref, head_ref, res_ref, top_ref, *refs):
    nb, steps, n_row, local_rows = cfg
    recv, out_ref, slots = refs[:n_row], refs[n_row], refs[n_row + 1]
    my_row = lax.axis_index("prow")
    slots[...] = jnp.zeros_like(slots)
    for k in range(n_row):
        slots[k * MOVE_SLOTS : k * MOVE_SLOTS + MOVE_ROWS, :] = recv[k][...]
    target = target_ref[...]
    for k in range(local_rows // nb):
        rows = slice(k * nb, (k + 1) * nb)
        hit = iota((nb, n_row * MOVE_SLOTS), 0) + k * nb == target
        moved = dot(one_hot(hit), slots[...]).astype(BF16)
        any_hit = jnp.sum(jnp.where(hit, 1.0, 0.0), axis=1, keepdims=True) > 0.5
        if k == 0:
            value = jnp.where(any_hit, moved, head_ref[...])
            value = jnp.where(my_row < steps, top_ref[...], value)
        else:
            value = jnp.where(any_hit, moved, res_ref[(k - 1) * nb : k * nb, :])
        out_ref[rows, :] = value


def call(kernel, outs, ins, scratch=(), any_at=(), flops=None):
    vmem = pl.BlockSpec(memory_space=pltpu.VMEM)
    anywhere = pl.BlockSpec(memory_space=pl.ANY)
    scalars = pl.BlockSpec(memory_space=pltpu.SMEM)
    return pl.pallas_call(
        kernel,
        out_shape=outs,
        in_specs=[
            jax.tree.map(lambda _: anywhere if i in any_at else vmem, x) for i, x in enumerate(ins)
        ],
        out_specs=jax.tree.map(lambda x: scalars if x.shape == (1,) else vmem, outs),
        scratch_shapes=list(scratch),
        compiler_params=pltpu.CompilerParams(vmem_limit_bytes=VMEM_BYTES),
        cost_estimate=flops
        and pl.CostEstimate(flops=flops, bytes_accessed=1 << 22, transcendentals=0),
    )(*ins)


def shape(*dims, dtype=BF16):
    return jax.ShapeDtypeStruct(dims, dtype)


def local(matrix, pivots, lower_inverse, upper_inverse):
    row_blocks, nb, col_blocks, _ = matrix.shape
    steps = pivots.shape[0]
    n_row = lax.axis_size("prow")
    n_col = lax.axis_size("pcol")
    if steps != 4 or col_blocks != 2 or n_row < steps or n_col < 8 or n_col % 4:
        return stepwise(matrix, pivots, lower_inverse, upper_inverse)
    local_rows = row_blocks * nb
    cap = -(-(steps * nb // n_row + 48) // 16) * 16
    mat = jnp.transpose(matrix, (2, 0, 1, 3)).reshape(col_blocks, local_rows, nb)
    m0 = mat[0]

    def from_panels(value, mask):
        return lax.ppermute(value, "pcol", [(i, i ^ mask) for i in range(steps)])

    def swap_cores(value):
        return lax.ppermute(value, "pcol", [(i, i ^ 1) for i in range(n_col)])

    def panel_pair(own, beside, far, far_beside):
        return jnp.where(on_panel, own, far), jnp.where(on_panel, beside, far_beside)

    on_panel = lax.axis_index("pcol") < steps
    fours = range(4, n_col, 4)
    meta, pack0, pack1 = call(
        functools.partial(pick_kernel, (nb, steps, n_row, cap, local_rows)),
        (shape(16, nb, dtype=I32), shape(cap, nb), shape(cap, nb)),
        (pivots, mat),
    )
    late0, pack0 = lax.optimization_barrier((m0, pack0))
    raw_x = from_panels(m0, 2)
    raw_far = functools.reduce(jnp.add, [from_panels(late0, mask) for mask in fours])
    parts = [pack0] + [
        lax.ppermute(pack0, "prow", [(i, (i + k) % n_row) for i in range(n_row)])
        for k in range(1, n_row)
    ]
    parts[1], raw_x = lax.optimization_barrier((parts[1], raw_x))
    raw_far_x = lax.ppermute(raw_far, "pcol", [(i, i ^ 2) for i in range(steps, n_col)])
    top0, off = call(
        functools.partial(order_kernel, (nb, steps, n_row, cap)),
        (shape(steps * nb, nb), shape((steps - 1) * nb, nb)),
        (meta, tuple(parts)),
        scratch=(pltpu.VMEM((n_row * cap, nb), BF16),),
    )
    pack1, off = lax.optimization_barrier((pack1, off))
    off_far = functools.reduce(jnp.add, [from_panels(off, mask) for mask in fours])
    off_x = from_panels(off, 2)
    off_far_x = functools.reduce(jnp.add, [from_panels(off, mask + 2) for mask in fours])
    buf1 = lax.all_gather(pack1, "prow", tiled=True)
    buf1, off_x, off_far_x, off_far = lax.optimization_barrier((buf1, off_x, off_far_x, off_far))
    raw_0, raw_2 = panel_pair(m0, raw_x, raw_far, raw_far_x)
    off_0, off_2 = panel_pair(off, off_x, off_far, off_far_x)
    raws = (raw_0, swap_cores(raw_0), raw_2, swap_cores(raw_2))
    offs = (off_0, swap_cores(off_0), off_2, swap_cores(off_2))
    top1 = call(
        functools.partial(second_kernel, (nb, steps, cap)), shape(steps * nb, nb), (meta, buf1)
    )
    top_rows = steps * nb
    upper, head, top, send = call(
        functools.partial(corner_kernel, (nb, steps, n_row)),
        (
            shape(top_rows, top_rows + 2 * nb), shape(nb, 2 * nb), shape(nb, 2 * nb),
            shape(n_row, MOVE_ROWS, 2 * nb),
        ),
        (pivots, top0, top1, mat, raws, offs, lower_inverse, upper_inverse),
        scratch=(
            pltpu.VMEM((steps, nb, nb), BF16),
            pltpu.VMEM((steps, top_rows - nb, nb), BF16),
            pltpu.VMEM((top_rows + nb, top_rows), BF16),
            pltpu.VMEM((top_rows, nb), BF16),
            pltpu.VMEM((steps, nb, nb), BF16),
            pltpu.SemaphoreType.DMA,
        ),
        any_at=(6,),
    )
    recv = [send[0]] + [
        lax.ppermute(send[k], "prow", [(i, (i + k) % n_row) for i in range(n_row)])
        for k in range(1, n_row)
    ]

    below = local_rows - nb
    res, target, crowded = call(
        functools.partial(rows_kernel, (nb, steps, n_row, cap, local_rows)),
        (
            shape(below, 2 * nb), shape(1, n_row * MOVE_SLOTS, dtype=I32), shape(1, dtype=I32),
        ),
        (pivots, meta, mat, raws, upper, upper_inverse),
        scratch=(
            pltpu.VMEM((steps, below, nb), BF16),
            pltpu.VMEM((below, top_rows), BF16),
            pltpu.VMEM((16, nb), I32),
        ),
        flops=2 * below * top_rows * (top_rows + 2 * nb),
    )

    def finish():
        out = call(
            functools.partial(place_kernel, (nb, steps, n_row, local_rows)),
            shape(local_rows, 2 * nb),
            (target, head, res, top, *recv),
            scratch=(pltpu.VMEM((n_row * MOVE_SLOTS, 2 * nb), BF16),),
        )
        return out.reshape(matrix.shape)

    return lax.cond(
        crowded[0] > 0,
        lambda: stepwise(matrix, pivots, lower_inverse, upper_inverse),
        finish,
    )


def solution(mesh):
    placed = (P(None, "prow", None, "pcol"), P(), P(), P())
    return jax.shard_map(
        local, mesh=mesh, in_specs=placed, out_specs=P(None, "prow", None, "pcol"), check_vma=False
    )
```

```python
import functools

import jax
import jax.numpy as jnp
from jax import lax
from jax.experimental import pallas as pl
from jax.experimental.pallas import tpu as pltpu
from jax.sharding import PartitionSpec as P

BF16 = jnp.bfloat16
F32 = jnp.float32
I32 = jnp.int32
VMEM_BYTES = 24 * 1024 * 1024
MOVE_ROWS = 64
MOVE_SLOTS = MOVE_ROWS


def ring_sum(value, axis):
    size = lax.axis_size(axis)

    def turn(_, carry):
        total, passing = carry
        passing = lax.ppermute(passing, axis, [(i, (i + 1) % size) for i in range(size)])
        return total + passing, passing

    return lax.fori_loop(1, size, turn, (value, value))[0]


def spread(value, axis, source):
    kept = jnp.where(lax.axis_index(axis) == source, value, 0).astype(value.dtype)
    return ring_sum(kept, axis)


def stepwise(matrix, pivots, lower_inverse, upper_inverse):
    row_blocks = matrix.shape[0]
    block_size = matrix.shape[1]
    col_blocks = matrix.shape[2]
    local_rows = row_blocks * block_size
    local_cols = col_blocks * block_size
    matrix_loc = matrix.reshape(local_rows, local_cols)
    row_count = lax.axis_size("prow")
    col_count = lax.axis_size("pcol")
    my_row = lax.axis_index("prow")
    my_col = lax.axis_index("pcol")
    row_iota = jnp.arange(local_rows, dtype=jnp.int32)
    col_iota = jnp.arange(local_cols, dtype=jnp.int32)
    global_row = (row_iota // block_size * row_count + my_row) * block_size + row_iota % block_size
    global_col = (col_iota // block_size * col_count + my_col) * block_size + col_iota % block_size
    for step_num in range(pivots.shape[0]):
        begin_at = step_num * block_size
        trail_at = begin_at + block_size
        diag_root = step_num % row_count
        diag_local = step_num // row_count * block_size
        panel_root = step_num % col_count
        panel_local = step_num // col_count * block_size
        targets = begin_at + jnp.arange(block_size, dtype=jnp.int32)
        chosen = pivots[step_num]
        chosen_block = chosen // block_size
        chosen_owner = chosen_block % row_count
        is_mine = chosen_owner == my_row
        chosen_local = chosen_block // row_count * block_size + chosen % block_size
        picked = jnp.take(matrix_loc, jnp.where(is_mine, chosen_local, 0), axis=0)
        picked = jnp.where(is_mine[:, None], picked, jnp.zeros_like(picked))
        diag_rows = matrix_loc[diag_local : diag_local + block_size]
        own_diag = jnp.where(my_row == diag_root, diag_rows, jnp.zeros_like(diag_rows))
        new_rows, old_diag = ring_sum(picked, "prow"), ring_sum(own_diag, "prow")
        moved_rows = is_mine & (chosen != targets)
        matrix_loc = matrix_loc.at[jnp.where(moved_rows, chosen_local, local_rows)].set(
            old_diag, mode="drop"
        )
        diag_after = matrix_loc[diag_local : diag_local + block_size]
        matrix_loc = matrix_loc.at[diag_local : diag_local + block_size].set(
            jnp.where(my_row == diag_root, new_rows, diag_after)
        )
        upper_full = jnp.dot(
            lower_inverse[step_num], new_rows, preferred_element_type=jnp.float32
        ).astype(jnp.bfloat16)
        col_live = global_col >= trail_at
        upper_use = jnp.where(col_live[None, :], upper_full, jnp.zeros_like(upper_full))
        panel_own = matrix_loc[:, panel_local : panel_local + block_size]
        received = spread(panel_own, "pcol", panel_root)
        left_full = jnp.dot(
            received, upper_inverse[step_num], preferred_element_type=jnp.float32
        ).astype(jnp.bfloat16)
        row_live = global_row >= trail_at
        left_use = jnp.where(row_live[:, None], left_full, jnp.zeros_like(left_full))
        matrix_loc = (
            matrix_loc.astype(jnp.float32)
            - jnp.dot(left_use, upper_use, preferred_element_type=jnp.float32)
        ).astype(jnp.bfloat16)
        panel_now = matrix_loc[:, panel_local : panel_local + block_size]
        panel_put = jnp.where(row_live[:, None] & (my_col == panel_root), left_full, panel_now)
        matrix_loc = matrix_loc.at[:, panel_local : panel_local + block_size].set(panel_put)
        diag_now = matrix_loc[diag_local : diag_local + block_size]
        diag_put = jnp.where(col_live[None, :] & (my_row == diag_root), upper_full, diag_now)
        matrix_loc = matrix_loc.at[diag_local : diag_local + block_size].set(diag_put)
    return matrix_loc.reshape(matrix.shape)


def iota(shape, dim):
    return lax.broadcasted_iota(I32, shape, dim)


def dot(a, b):
    return jnp.dot(a, b, preferred_element_type=F32)


def one_hot(hit):
    return jnp.where(hit, 1.0, 0.0).astype(BF16)


def to_col(row, size):
    eye = iota((size, size), 0) == iota((size, size), 1)
    return jnp.sum(jnp.where(eye, jnp.broadcast_to(row, (size, size)), 0), axis=1, keepdims=True)


def find(col, base, x, size):
    hit = col == x
    place = jnp.sum(jnp.where(hit, iota((size, size), 0) + (base + 1), 0), axis=0, keepdims=True)
    return jnp.where(place > 0, place - 1, x)


def look(col, base, x, size):
    hit = iota((size, size), 0) + base == x
    return jnp.sum(jnp.where(hit, col, 0), axis=0, keepdims=True)


def before(rows, size):
    tri = one_hot(iota((size, size), 0) < iota((size, size), 1))
    stacked = jnp.concatenate([one_hot(r) for r in rows], axis=0)
    counts = dot(stacked, tri)
    k = rows[0].shape[0]
    return [counts[i * k : (i + 1) * k] for i in range(len(rows))]


def pick_kernel(cfg, piv_ref, mat_ref, meta_ref, pack0_ref, pack1_ref):
    nb, steps, n_row, cap, local_rows = cfg
    my_row = lax.axis_index("prow")
    piv = [piv_ref[t : t + 1, :] for t in range(steps)]
    cols = [to_col(piv[t], nb) for t in range(steps - 1)]
    owners, places = [], []
    for t in range(steps):
        x = piv[t]
        for s in range(t - 1, -1, -1):
            x = find(cols[s], s * nb, x, nb)
        block = x // nb
        owners.append(block % n_row)
        places.append(block // n_row * nb + x % nb)
    lanes = -(-n_row // 8) * 8
    member = [iota((lanes, nb), 0) == w for w in owners]
    counts = before(member, nb)
    base = jnp.zeros((lanes, 1), F32)
    ranks = []
    for t in range(steps):
        ranks.append(
            jnp.sum(jnp.where(member[t], counts[t] + base, 0.0), axis=0, keepdims=True).astype(I32)
        )
        base = base + jnp.sum(jnp.where(member[t], 1.0, 0.0), axis=1, keepdims=True)
    for t in range(steps):
        meta_ref[t : t + 1, :] = owners[t]
        meta_ref[steps + t : steps + t + 1, :] = ranks[t]
    over = jnp.max(base, axis=0, keepdims=True).astype(I32)
    meta_ref[2 * steps : 2 * steps + 1, :] = jnp.broadcast_to(over, (1, nb))
    slot = iota((cap, nb), 0)
    total = jnp.zeros((cap, nb), I32)
    for t in range(steps):
        key = jnp.where(owners[t] == my_row, ranks[t], -1)
        total = total + jnp.where(slot == key, places[t] + 1, 0)
    source = jnp.sum(total, axis=1, keepdims=True) - 1
    chosen = one_hot(source == iota((cap, local_rows), 1))
    pack0_ref[...] = dot(chosen, mat_ref[0]).astype(BF16)
    pack1_ref[...] = dot(chosen, mat_ref[1]).astype(BF16)


def final_places(x, cols, steps, size):
    for s in steps:
        base = s * size
        inside = (x >= base) & (x < base + size)
        x = jnp.where(inside, look(cols[s], base, x, size), find(cols[s], base, x, size))
    return x


def find_moves(cfg, piv_ref, meta_ref, move_ref):
    nb, steps, n_row, cap = cfg
    cols = [to_col(piv_ref[t : t + 1, :], nb) for t in range(steps)]
    lanes = -(-n_row // 8) * 8
    member = []
    for t in range(steps):
        at = iota((1, nb), 1) + t * nb
        x = at
        for s in range(t):
            x = find(cols[s], s * nb, x, nb)
        x = jnp.where(x == at, piv_ref[t : t + 1, :], x)
        x = final_places(x, cols, range(t + 1, steps), nb)
        block = x // nb
        dest = jnp.where(x >= steps * nb, block % n_row, -1)
        move_ref[t : t + 1, :] = dest
        move_ref[2 * steps + t : 2 * steps + t + 1, :] = block // n_row * nb + x % nb
        member.append(iota((lanes, nb), 0) == dest)
    counts = before(member, nb)
    most = jnp.zeros((lanes, 1), F32)
    for t in range(steps):
        move_ref[steps + t : steps + t + 1, :] = jnp.sum(
            jnp.where(member[t], counts[t], 0.0), axis=0, keepdims=True
        ).astype(I32)
        most = jnp.maximum(most, jnp.sum(jnp.where(member[t], 1.0, 0.0), axis=1, keepdims=True))
    over = jnp.max(most, axis=0, keepdims=True).astype(I32)
    bad = (over > MOVE_ROWS) | (meta_ref[2 * steps : 2 * steps + 1, :] > cap)
    return jnp.where(bad, 1, 0)


def find_targets(cfg, move_ref, my_row):
    nb, steps, n_row = cfg
    targets = []
    for k in range(n_row):
        here = iota((steps, nb), 0) == lax.rem(my_row + n_row - k, n_row)
        dest = jnp.sum(jnp.where(here, move_ref[:steps, :] + 1, 0), axis=0, keepdims=True) - 1
        rank = jnp.sum(jnp.where(here, move_ref[steps : 2 * steps, :], 0), axis=0, keepdims=True)
        place = jnp.sum(
            jnp.where(here, move_ref[2 * steps : 3 * steps, :], 0), axis=0, keepdims=True
        )
        key = jnp.where(dest == my_row, rank, -1)
        hot = one_hot(key == iota((MOVE_SLOTS, nb), 0))
        row = iota((8, nb), 0)
        parts = jnp.where(row == 0, place // 128, jnp.where(row == 1, place % 128, 1))
        found = lax.dot_general(
            parts.astype(F32).astype(BF16), hot, (((1,), (1,)), ((), ())),
            preferred_element_type=F32,
        )
        at = found[0:1] * 128.0 + found[1:2]
        targets.append(jnp.where(found[2:3] > 0.5, at, -1.0).astype(I32))
    return jnp.concatenate(targets, axis=1)


def order_rows(pos, buf_ref):
    nb = pos.shape[1]
    hot = one_hot(to_col(pos, nb) == iota((nb, buf_ref.shape[0]), 1))
    return dot(hot, buf_ref[...]).astype(BF16)


def order_kernel(cfg, meta_ref, parts, top_ref, off_ref, buf):
    nb, steps, n_row, cap = cfg
    my_row = lax.axis_index("prow")
    my_col = lax.axis_index("pcol")
    for k in range(n_row):
        buf[k * cap : (k + 1) * cap, :] = parts[k][...]
    for t in range(steps):
        turn = my_row - meta_ref[t : t + 1, :]
        turn = jnp.where(turn < 0, turn + n_row, turn)
        pos = turn * cap + meta_ref[steps + t : steps + t + 1, :]
        top_ref[t * nb : (t + 1) * nb, :] = order_rows(pos, buf)
    for j in range(steps - 1):
        block = jnp.where(my_col <= j, j + 1, j)
        rows = pl.ds(pl.multiple_of(block * nb, nb), nb)
        off_ref[j * nb : (j + 1) * nb, :] = top_ref[rows, :]


def second_kernel(cfg, meta_ref, buf_ref, top_ref):
    nb, steps, cap = cfg
    for t in range(steps):
        pos = meta_ref[t : t + 1, :] * cap + meta_ref[steps + t : steps + t + 1, :]
        top_ref[t * nb : (t + 1) * nb, :] = order_rows(pos, buf_ref)


def sort_panels(panels, into, rows):
    low = lax.axis_index("pcol") & 3
    for mask, panel in enumerate(panels):
        into[low ^ mask] = panel[rows, :]


def corner_kernel(
    cfg, piv_ref, top0_ref, top1_ref, mat_ref, raws, offs, linv_hbm, uinv_ref,
    upper, res_ref, top_ref, send_ref, raw, off, left, diag, linv_ref, sem,
):
    nb, steps, n_row = cfg
    wide = steps * nb
    my_row = lax.axis_index("prow")
    my_col = lax.axis_index("pcol")
    load = pltpu.make_async_copy(linv_hbm, linv_ref, sem)
    load.start()
    sort_panels(offs, off, slice(0, wide - nb))
    sort_panels(raws, raw, slice(0, nb))
    load.wait()
    for t in range(steps):
        here = slice(t * nb, (t + 1) * nb)
        done = slice(0, t * nb)
        parts = [off[j, here, :] for j in range(t + 1, steps)]
        parts += [top0_ref[here, :], top1_ref[here, :]]
        column = [off[t, t * nb :, :]] if t < steps - 1 else []
        column += [raw[t]]
        if t > 0:
            prod = dot(left[here, done], upper[done, (t + 1) * nb :])
            parts = [
                (p.astype(F32) - prod[:, i * nb : (i + 1) * nb]).astype(BF16)
                for i, p in enumerate(parts)
            ]
            prod = dot(left[(t + 1) * nb :, done], upper[done, here])
            at = 0
            for i, p in enumerate(column):
                rows = p.shape[0]
                column[i] = (p.astype(F32) - prod[at : at + rows]).astype(BF16)
                at += rows
        diag[here, :] = parts[-2]
        upper[here, (t + 1) * nb :] = dot(linv_ref[t], jnp.concatenate(parts, axis=1)).astype(BF16)
        left[(t + 1) * nb :, here] = dot(jnp.concatenate(column, axis=0), uinv_ref[t]).astype(BF16)
    in_panel = my_col < steps
    panel = pl.ds(pl.multiple_of(jnp.minimum(my_col, steps - 1) * nb, nb), nb)
    prod = dot(left[wide:, :], upper[:, wide:])
    value = (mat_ref[0, :nb, :].astype(F32) - prod[:, :nb]).astype(BF16)
    res_ref[:, :nb] = jnp.where(in_panel, left[wide:, panel], value)
    res_ref[:, nb:] = (mat_ref[1, :nb, :].astype(F32) - prod[:, nb:]).astype(BF16)
    cols = [to_col(piv_ref[t : t + 1, :], nb) for t in range(steps)]
    x = final_places(iota((1, nb), 1) + my_row * nb, cols, range(steps), nb)
    dest = jnp.where((x >= wide) & (my_row < steps), x // nb % n_row, -1)
    member = iota((-(-n_row // 8) * 8, nb), 0) == dest
    rank = jnp.sum(jnp.where(member, before([member], nb)[0], 0.0), axis=0, keepdims=True)
    rank = rank.astype(I32)
    hot = []
    for k in range(n_row):
        key = jnp.where(dest == lax.rem(my_row + k, n_row), rank, -1)
        hot.append(one_hot(key == iota((MOVE_ROWS, nb), 0)))
    moved = dot(jnp.concatenate(hot, axis=0), res_ref[...]).astype(BF16)
    for k in range(n_row):
        send_ref[k] = moved[k * MOVE_ROWS : (k + 1) * MOVE_ROWS]
    block = pl.ds(pl.multiple_of(jnp.minimum(my_row, steps - 1) * nb, nb), nb)
    value = jnp.where(my_col == my_row, diag[block, :], upper[block, wide : wide + nb])
    value = jnp.where(in_panel & (my_col < my_row), left[block, panel], value)
    top_ref[:, :nb] = value
    top_ref[:, nb:] = upper[block, wide + nb :]


def rows_kernel(
    cfg, piv_ref, meta_ref, mat_ref, raws, upper, uinv_ref, res_ref, target_ref,
    flag_ref, raw, l_own, move_ref,
):
    nb, steps, n_row, cap, local_rows = cfg
    my_col = lax.axis_index("pcol")
    sort_panels(raws, raw, slice(nb, local_rows))
    bad = find_moves((nb, steps, n_row, cap), piv_ref, meta_ref, move_ref)
    target_ref[...] = find_targets((nb, steps, n_row), move_ref, lax.axis_index("prow"))
    flag_ref[0] = jnp.max(bad)
    tiles = [slice(0, local_rows - nb)]
    for t in range(steps):
        here = slice(t * nb, (t + 1) * nb)
        done = slice(0, t * nb)
        for rows in tiles:
            acc = raw[t, rows, :].astype(F32)
            if t > 0:
                acc = acc - dot(l_own[rows, done], upper[done, here])
            l_own[rows, here] = dot(acc.astype(BF16), uinv_ref[t]).astype(BF16)
    in_panel = my_col < steps
    panel = pl.ds(pl.multiple_of(jnp.minimum(my_col, steps - 1) * nb, nb), nb)
    for rows in tiles:
        prod = dot(l_own[rows, :], upper[:, steps * nb :])
        source = slice(rows.start + nb, rows.stop + nb)
        left = (mat_ref[0, source, :].astype(F32) - prod[:, :nb]).astype(BF16)
        res_ref[rows, :nb] = jnp.where(in_panel, l_own[rows, panel], left)
        res_ref[rows, nb:] = (mat_ref[1, source, :].astype(F32) - prod[:, nb:]).astype(BF16)


def place_kernel(cfg, target_ref, head_ref, res_ref, top_ref, *refs):
    nb, steps, n_row, local_rows = cfg
    recv, out_ref, slots = refs[:n_row], refs[n_row], refs[n_row + 1]
    my_row = lax.axis_index("prow")
    for k in range(n_row):
        slots[k * MOVE_SLOTS : k * MOVE_SLOTS + MOVE_ROWS, :] = recv[k][...]
    target = target_ref[...]
    for k in range(local_rows // nb):
        rows = slice(k * nb, (k + 1) * nb)
        hit = iota((nb, n_row * MOVE_SLOTS), 0) + k * nb == target
        moved = dot(one_hot(hit), slots[...]).astype(BF16)
        any_hit = jnp.sum(jnp.where(hit, 1.0, 0.0), axis=1, keepdims=True) > 0.5
        if k == 0:
            value = jnp.where(any_hit, moved, head_ref[...])
            value = jnp.where(my_row < steps, top_ref[...], value)
        else:
            value = jnp.where(any_hit, moved, res_ref[(k - 1) * nb : k * nb, :])
        out_ref[rows, :] = value


def call(kernel, outs, ins, scratch=(), any_at=(), flops=None):
    vmem = pl.BlockSpec(memory_space=pltpu.VMEM)
    anywhere = pl.BlockSpec(memory_space=pl.ANY)
    scalars = pl.BlockSpec(memory_space=pltpu.SMEM)
    return pl.pallas_call(
        kernel,
        out_shape=outs,
        in_specs=[
            jax.tree.map(lambda _: anywhere if i in any_at else vmem, x) for i, x in enumerate(ins)
        ],
        out_specs=jax.tree.map(lambda x: scalars if x.shape == (1,) else vmem, outs),
        scratch_shapes=list(scratch),
        compiler_params=pltpu.CompilerParams(vmem_limit_bytes=VMEM_BYTES),
        cost_estimate=flops
        and pl.CostEstimate(flops=flops, bytes_accessed=1 << 22, transcendentals=0),
    )(*ins)


def shape(*dims, dtype=BF16):
    return jax.ShapeDtypeStruct(dims, dtype)


def local(matrix, pivots, lower_inverse, upper_inverse):
    row_blocks, nb, col_blocks, _ = matrix.shape
    steps = pivots.shape[0]
    n_row = lax.axis_size("prow")
    n_col = lax.axis_size("pcol")
    if steps != 4 or col_blocks != 2 or n_row < steps or n_col < 8 or n_col % 4:
        return stepwise(matrix, pivots, lower_inverse, upper_inverse)
    local_rows = row_blocks * nb
    cap = -(-(steps * nb // n_row + 48) // 16) * 16
    mat = jnp.transpose(matrix, (2, 0, 1, 3)).reshape(col_blocks, local_rows, nb)
    m0 = mat[0]

    def from_panels(value, mask):
        return lax.ppermute(value, "pcol", [(i, i ^ mask) for i in range(steps)])

    def swap_cores(value):
        return lax.ppermute(value, "pcol", [(i, i ^ 1) for i in range(n_col)])

    def panel_pair(own, beside, far, far_beside):
        return jnp.where(on_panel, own, far), jnp.where(on_panel, beside, far_beside)

    on_panel = lax.axis_index("pcol") < steps
    fours = range(4, n_col, 4)
    meta, pack0, pack1 = call(
        functools.partial(pick_kernel, (nb, steps, n_row, cap, local_rows)),
        (shape(16, nb, dtype=I32), shape(cap, nb), shape(cap, nb)),
        (pivots, mat),
    )
    late0, pack0 = lax.optimization_barrier((m0, pack0))
    raw_x = from_panels(m0, 2)
    raw_far = functools.reduce(jnp.add, [from_panels(late0, mask) for mask in fours])
    parts = [pack0] + [
        lax.ppermute(pack0, "prow", [(i, (i + k) % n_row) for i in range(n_row)])
        for k in range(1, n_row)
    ]
    parts[1], raw_x = lax.optimization_barrier((parts[1], raw_x))
    raw_far_x = lax.ppermute(raw_far, "pcol", [(i, i ^ 2) for i in range(steps, n_col)])
    top0, off = call(
        functools.partial(order_kernel, (nb, steps, n_row, cap)),
        (shape(steps * nb, nb), shape((steps - 1) * nb, nb)),
        (meta, tuple(parts)),
        scratch=(pltpu.VMEM((n_row * cap, nb), BF16),),
    )
    pack1, off = lax.optimization_barrier((pack1, off))
    off_far = functools.reduce(jnp.add, [from_panels(off, mask) for mask in fours])
    off_x = from_panels(off, 2)
    off_far_x = functools.reduce(jnp.add, [from_panels(off, mask + 2) for mask in fours])
    buf1 = lax.all_gather(pack1, "prow", tiled=True)
    buf1, off_x, off_far_x, off_far = lax.optimization_barrier((buf1, off_x, off_far_x, off_far))
    raw_0, raw_2 = panel_pair(m0, raw_x, raw_far, raw_far_x)
    off_0, off_2 = panel_pair(off, off_x, off_far, off_far_x)
    raws = (raw_0, swap_cores(raw_0), raw_2, swap_cores(raw_2))
    offs = (off_0, swap_cores(off_0), off_2, swap_cores(off_2))
    top1 = call(
        functools.partial(second_kernel, (nb, steps, cap)), shape(steps * nb, nb), (meta, buf1)
    )
    top_rows = steps * nb
    upper, head, top, send = call(
        functools.partial(corner_kernel, (nb, steps, n_row)),
        (
            shape(top_rows, top_rows + 2 * nb), shape(nb, 2 * nb), shape(nb, 2 * nb),
            shape(n_row, MOVE_ROWS, 2 * nb),
        ),
        (pivots, top0, top1, mat, raws, offs, lower_inverse, upper_inverse),
        scratch=(
            pltpu.VMEM((steps, nb, nb), BF16),
            pltpu.VMEM((steps, top_rows - nb, nb), BF16),
            pltpu.VMEM((top_rows + nb, top_rows), BF16),
            pltpu.VMEM((top_rows, nb), BF16),
            pltpu.VMEM((steps, nb, nb), BF16),
            pltpu.SemaphoreType.DMA,
        ),
        any_at=(6,),
    )
    recv = [send[0]] + [
        lax.ppermute(send[k], "prow", [(i, (i + k) % n_row) for i in range(n_row)])
        for k in range(1, n_row)
    ]

    below = local_rows - nb
    res, target, crowded = call(
        functools.partial(rows_kernel, (nb, steps, n_row, cap, local_rows)),
        (
            shape(below, 2 * nb), shape(1, n_row * MOVE_SLOTS, dtype=I32), shape(1, dtype=I32),
        ),
        (pivots, meta, mat, raws, upper, upper_inverse),
        scratch=(
            pltpu.VMEM((steps, below, nb), BF16),
            pltpu.VMEM((below, top_rows), BF16),
            pltpu.VMEM((16, nb), I32),
        ),
        flops=2 * below * top_rows * (top_rows + 2 * nb),
    )

    def finish():
        out = call(
            functools.partial(place_kernel, (nb, steps, n_row, local_rows)),
            shape(local_rows, 2 * nb),
            (target, head, res, top, *recv),
            scratch=(pltpu.VMEM((n_row * MOVE_SLOTS, 2 * nb), BF16),),
        )
        return out.reshape(matrix.shape)

    return lax.cond(
        crowded[0] > 0,
        lambda: stepwise(matrix, pivots, lower_inverse, upper_inverse),
        finish,
    )


def solution(mesh):
    placed = (P(None, "prow", None, "pcol"), P(), P(), P())
    return jax.shard_map(
        local, mesh=mesh, in_specs=placed, out_specs=P(None, "prow", None, "pcol"), check_vma=False
    )
```
